512 devices in a mesh: gx: 64 (over x_lo, z, core), gy: 8 (over x_hi, y).
Axes of the slice: x: 4 (x_hi: 2, x_lo: 2; x = x_hi * 2 + x_lo), y: 4, z: 16, core: 2. Of those that a mesh axis runs over, the one named last changes fastest.
Arguments:
- features: bfloat16 [512, 64, 1, 8, 128], P('gx', 'gy'), may hold values from -6 to 6
- occupancy: int32 [512, 64, 1], P('gx', 'gy'), may hold values from 0 to 255
- neighbours: int32 [64, 8, 1, 27], P('gx', 'gy'), may hold values from -1 to 0, as said below
- first_weight: bfloat16 [27, 128, 128], replicated, may hold values from -0.109375 to 0.109375
- second_weight: bfloat16 [27, 128, 128], replicated, may hold values from -0.109375 to 0.109375
- cotangent: bfloat16 [512, 64, 1, 8, 128], P('gx', 'gy'), may hold values from -6 to 6
Outputs:
- activations: bfloat16 [512, 64, 1, 8, 128], P('gx', 'gy')
- first_grad: bfloat16 [27, 128, 128], replicated
- second_grad: bfloat16 [27, 128, 128], replicated
The draws below stay inside these ranges and needn't reach their ends.
Inputs may be any that keep to these rules, and one draw needn't show every extreme that they name: `occupancy`: bit k of an entry says whether voxel layer k of that block row is occupied. `neighbours`: entry 9 (i + 1) + 3 (j + 1) + (l + 1) of slot t in column (a, b) names the slot of column (a + i, b + j) whose block lies l block layers above slot t's block, or -1 when no active block is there, the column lies outside the grid, or slot t is empty. Entry 13 is t for an active slot and -1 for an empty one; active slots come first in a column; the blocks of a column lie at distinct layers among 8; in every draw some column has all 1 slots active.
All inputs are finite; a program needn't handle non-finite values.
Results may differ from the reference program's by a relative error of at most 0.0054.
Values may be sent and summed in bfloat16 or wider, within the bound.
No kernel may reach another device: no remote copies, remote signals or barrier semaphores. Data moves between devices by JAX's collectives and lax.ppermute only.
A program may use at most 64 MiB of HBM per device.

```python
import math
import jax
import jax.numpy as jnp
from jax import lax

C = 128
BLOCK = 8
BZ = 8
SLOTS = 1
COLX = 64
COLY = 8
VX = 512
VY = 64


def draw_neighbours(key, part):
    key = jax.random.fold_in(key, 11)
    level_key, full_key, layer_key = jax.random.split(key, 3)
    column_count = COLX * COLY
    levels = jax.random.randint(level_key, (column_count,), 0, 10)
    counts = jnp.where(levels < 6, 1, jnp.where(levels < 9, 2, 3))
    counts = jnp.minimum(counts, SLOTS)
    chosen = jax.random.randint(full_key, (), 0, column_count)
    counts = jnp.where(jnp.arange(column_count) == chosen, SLOTS, counts)
    layer_keys = jax.random.split(layer_key, column_count)
    layers = jax.vmap(lambda single: jax.random.permutation(single, BZ))(layer_keys)[:, :SLOTS].astype(jnp.int32)
    active = jnp.arange(SLOTS)[None, :] < counts[:, None]
    heights = jnp.where(active, layers, -1).reshape(COLX, COLY, SLOTS)
    padded = jnp.pad(heights, ((1, 1), (1, 1), (0, 0)), constant_values=-1)
    numbers = jnp.arange(1, SLOTS + 1, dtype=jnp.int32)
    entries = []
    for x_shift in range(3):
        for y_shift in range(3):
            for z_shift in range(3):
                nearby = padded[x_shift:x_shift + COLX, y_shift:y_shift + COLY]
                target = heights + (z_shift - 1)
                match = (nearby[:, :, None, :] == target[:, :, :, None]) & (heights[:, :, :, None] >= 0) & (nearby[:, :, None, :] >= 0)
                entries.append(jnp.sum(jnp.where(match, numbers, 0), axis=-1) - 1)
    return jnp.stack(entries, axis=-1).astype(jnp.int32)


def touch_ends(array, key, least, largest):
    spot = [jax.random.randint(jax.random.fold_in(key, axis), (), 0, length) for axis, length in enumerate(array.shape)]
    main_axis = array.shape.index(max(array.shape))
    beside = spot[:main_axis] + [(spot[main_axis] + 1) % array.shape[main_axis]] + spot[main_axis + 1:]
    return array.at[tuple(spot)].set(least).at[tuple(beside)].set(largest)


def steps_of(rng, dims, cuts, smallest, largest):
    def one(dim, shards_of):
        steps = jax.random.uniform(jax.random.fold_in(jax.random.fold_in(rng, 6), dim), (shards_of,), jnp.float32, smallest / len(cuts), largest / len(cuts))
        return jnp.repeat(jnp.exp(steps), dims[dim] // shards_of).reshape((-1,) + (1,) * (len(dims) - dim - 1))

    gain = one(*cuts[0])
    for cut in cuts[1:]:
        gain = gain * one(*cut)
    return gain


def centred(key, shape, scale, reach, pieces=(), kind=jnp.bfloat16):
    values = jax.random.normal(key, shape, jnp.float32) * scale
    if len(pieces) > 0:
        values = steps_of(key, shape, pieces, -0.22, 0.18) * values
    return jnp.clip(values, min=-reach, max=reach).astype(kind)


def setup_inputs(seed: int = 0) -> dict:
    keys = jax.random.split(jax.random.key(seed), 7)
    features = centred(keys[0], (VX, VY, SLOTS, BLOCK, C), 1.0, 6.0, ((0, 64), (1, 8)))
    occupancy = touch_ends(jax.random.randint(keys[1], (VX, VY, SLOTS), 0, 2 ** BLOCK), jax.random.fold_in(keys[1], 1), 0, (2 ** BLOCK) - 1).astype(jnp.int32)
    neighbours = draw_neighbours(jax.random.fold_in(keys[6], 71), 0)
    first_weight = centred(keys[3], (27, C, C), (27 * C) ** -0.5, 0.109375)
    second_weight = centred(keys[4], (27, C, C), (27 * C) ** -0.5, 0.109375)
    cotangent = centred(keys[5], (VX, VY, SLOTS, BLOCK, C), 1.0, 6.0, ((0, 64), (1, 8)))
    return {"features": features, "occupancy": occupancy, "neighbours": neighbours, "first_weight": first_weight, "second_weight": second_weight, "cotangent": cotangent}


def extend(window, lookup):
    extent = window.shape[0] - 2
    side_ranges = [(0, 1), (1, extent + 1), (extent + 1, extent + 2)]
    z_ranges = [(extent - 1, extent), (0, extent), (0, 1)]
    x_parts = []
    for x_part in range(3):
        y_parts = []
        for y_part in range(3):
            region = window[side_ranges[x_part][0]:side_ranges[x_part][1], side_ranges[y_part][0]:side_ranges[y_part][1]]
            z_parts = []
            for z_part in range(3):
                source = lookup[:, 9 * x_part + 3 * y_part + z_part]
                layers = region[:, :, :, z_ranges[z_part][0]:z_ranges[z_part][1]]
                gathered = jnp.take(layers, jnp.maximum(source, 0), axis=2)
                present = (source >= 0).astype(window.dtype)
                z_parts.append(gathered * present[None, None, :, None, None])
            y_parts.append(jnp.concatenate(z_parts, axis=3))
        x_parts.append(jnp.concatenate(y_parts, axis=1))
    return jnp.concatenate(x_parts, axis=0)

def gather_taps(extended):
    extent = extended.shape[3] - 2
    columns = []
    for x_shift in range(3):
        for y_shift in range(3):
            for z_shift in range(3):
                columns.append(extended[x_shift:x_shift + extent, y_shift:y_shift + extent, :, z_shift:z_shift + extent, :])
    return jnp.concatenate(columns, axis=-1)

def flat_product(patches, weight):
    shape = patches.shape
    result = jnp.dot(patches.reshape(-1, shape[-1]), weight, preferred_element_type=jnp.float32)
    return result.reshape(shape[:-1] + (weight.shape[1],))

def outer_sum(patches, grads):
    return lax.dot_general(patches.reshape(-1, patches.shape[-1]), grads.reshape(-1, grads.shape[-1]), (((0,), (0,)), ((), ())), preferred_element_type=jnp.float32)

def silu_slope(pre):
    logistic = jax.nn.sigmoid(pre)
    return logistic * (1.0 + pre * (1.0 - logistic))

def occupancy_mask(occupancy, live_cells, extent):
    bit_values = jnp.right_shift(occupancy[..., None], jnp.arange(extent, dtype=jnp.int32)) & 1
    return (bit_values * live_cells[..., None].astype(jnp.int32)).astype(jnp.bfloat16)

def reference(features, occupancy, neighbours, first_weight, second_weight, cotangent):
    channels = features.shape[-1]
    live = neighbours[..., 13] >= 0
    live_cells = jnp.repeat(jnp.repeat(live, BLOCK, axis=0), BLOCK, axis=1)
    mask = occupancy_mask(occupancy, live_cells, BLOCK)
    masked = features * mask[..., None]
    grad_out = cotangent * mask[..., None]
    first_flat = first_weight.reshape(27 * channels, channels)
    second_flat = second_weight.reshape(27 * channels, channels)
    second_back = jnp.transpose(second_weight[::-1], (0, 2, 1)).reshape(27 * channels, channels)
    column_count = COLX * COLY
    tables = neighbours.reshape(column_count, SLOTS, 27)
    indices = jnp.arange(column_count, dtype=jnp.int32)
    zero_start = jnp.zeros((), jnp.int32)
    widths = ((1, 1), (1, 1), (0, 0), (0, 0), (0, 0))

    def corner_of(index, rank):
        x_column = (index // COLY).astype(jnp.int32)
        y_column = (index % COLY).astype(jnp.int32)
        return (x_column * BLOCK, y_column * BLOCK) + (zero_start,) * (rank - 2)

    def window_of(padded, index):
        return lax.dynamic_slice(padded, corner_of(index, padded.ndim), (BLOCK + 2, BLOCK + 2) + padded.shape[2:])

    def own_block(volume, index):
        return lax.dynamic_slice(volume, corner_of(index, volume.ndim), (BLOCK, BLOCK) + volume.shape[2:])

    def assemble(stacked):
        shaped = stacked.reshape((COLX, COLY, BLOCK, BLOCK) + stacked.shape[3:])
        shaped = jnp.transpose(shaped, (0, 2, 1, 3, 4, 5, 6))
        return shaped.reshape((COLX * BLOCK, COLY * BLOCK) + stacked.shape[3:])
    pad_masked = jnp.pad(masked, widths)

    def first_forward(index):
        patches = gather_taps(extend(window_of(pad_masked, index), tables[index]))
        return flat_product(patches, first_flat)
    pre_first = assemble(lax.map(first_forward, indices))
    hidden = (jax.nn.silu(pre_first) * mask[..., None]).astype(jnp.bfloat16)
    pad_hidden = jnp.pad(hidden, widths)

    def second_step(total, index):
        patches = gather_taps(extend(window_of(pad_hidden, index), tables[index]))
        grads = own_block(grad_out, index)
        return (total + outer_sum(patches, grads), flat_product(patches, second_flat))
    empty = jnp.zeros((27 * channels, channels), jnp.float32)
    second_total, stacked = lax.scan(second_step, empty, indices)
    activations = (assemble(stacked) * mask[..., None]).astype(jnp.bfloat16)
    pad_grad = jnp.pad(grad_out, widths)

    def first_step(total, index):
        back = flat_product(gather_taps(extend(window_of(pad_grad, index), tables[index])), second_back)
        pre = own_block(pre_first, index)
        local_mask = own_block(mask, index)
        grad_pre = (back * silu_slope(pre) * local_mask[..., None]).astype(jnp.bfloat16)
        patches = gather_taps(extend(window_of(pad_masked, index), tables[index]))
        return (total + outer_sum(patches, grad_pre), None)
    first_total, unused = lax.scan(first_step, empty, indices)
    scale = 1.0 / math.sqrt(BLOCK ** 3 * SLOTS * COLX * COLY)
    first_grad = (first_total * scale).reshape(27, channels, channels).astype(jnp.bfloat16)
    second_grad = (second_total * scale).reshape(27, channels, channels).astype(jnp.bfloat16)
    return (activations, first_grad, second_grad)
```

```python
import math

import jax
import jax.numpy as jnp
from jax import lax
from jax.sharding import Mesh
from jax.sharding import PartitionSpec as P

GX = ("x_lo", "z", "core")
GY = ("x_hi", "y")


def padded(array, sides, width):
    for axis, dim in sides:
        count, length = (lax.axis_size(axis), array.shape[dim])
        up = [(i, (i + 1) % count) for i in range(count - 1)]
        down = [(j, i) for i, j in up]
        last = lax.slice_in_dim(array, length - width, length, axis=dim)
        first = lax.slice_in_dim(array, 0, width, axis=dim)
        before = lax.ppermute(last, axis, up)
        after = lax.ppermute(first, axis, down)
        array = jnp.concatenate([before, array, after], axis=dim)
    return array


def extend(window, lookup):
    extent = window.shape[0] - 2
    side_ranges = [(0, 1), (1, extent + 1), (extent + 1, extent + 2)]
    z_ranges = [(extent - 1, extent), (0, extent), (0, 1)]
    x_parts = []
    for x_part in range(3):
        y_parts = []
        for y_part in range(3):
            region = window[
                side_ranges[x_part][0] : side_ranges[x_part][1],
                side_ranges[y_part][0] : side_ranges[y_part][1],
            ]
            z_parts = []
            for z_part in range(3):
                source = lookup[:, 9 * x_part + 3 * y_part + z_part]
                layers = region[:, :, :, z_ranges[z_part][0] : z_ranges[z_part][1]]
                gathered = jnp.take(layers, jnp.maximum(source, 0), axis=2)
                present = (source >= 0).astype(window.dtype)
                z_parts.append(gathered * present[None, None, :, None, None])
            y_parts.append(jnp.concatenate(z_parts, axis=3))
        x_parts.append(jnp.concatenate(y_parts, axis=1))
    return jnp.concatenate(x_parts, axis=0)


def gather_taps(extended):
    extent = extended.shape[3] - 2
    columns = []
    for x_shift in range(3):
        for y_shift in range(3):
            for z_shift in range(3):
                columns.append(
                    extended[
                        x_shift : x_shift + extent,
                        y_shift : y_shift + extent,
                        :,
                        z_shift : z_shift + extent,
                        :,
                    ]
                )
    return jnp.concatenate(columns, axis=-1)


def flat_product(patches, weight):
    shape = patches.shape
    result = jnp.dot(patches.reshape(-1, shape[-1]), weight, preferred_element_type=jnp.float32)
    return result.reshape(shape[:-1] + (weight.shape[1],))


def outer_sum(patches, grads):
    return lax.dot_general(
        patches.reshape(-1, patches.shape[-1]),
        grads.reshape(-1, grads.shape[-1]),
        (((0,), (0,)), ((), ())),
        preferred_element_type=jnp.float32,
    )


def silu_slope(pre):
    logistic = jax.nn.sigmoid(pre)
    return logistic * (1.0 + pre * (1.0 - logistic))


def occupancy_mask(occupancy, live_cells, extent):
    bit_values = jnp.right_shift(occupancy[..., None], jnp.arange(extent, dtype=jnp.int32)) & 1
    return (bit_values * live_cells[..., None].astype(jnp.int32)).astype(jnp.bfloat16)


def boundary(volume):
    return padded(volume, ((GX, 0), (GY, 1)), 1)


def exchange(parts, axes):
    return lax.all_to_all(parts, axes, 0, 0, tiled=True)


def summed(parts):
    return jnp.sum(parts.astype(jnp.float32), axis=0).astype(jnp.bfloat16)


def shared(part, count):
    return jnp.broadcast_to(part[None], (count,) + part.shape)


def reduced(first_total, second_total, scale):
    core = lax.axis_index("core")
    swap = [(0, 1), (1, 0)]
    plane = ("x_lo", "x_hi", "y")
    along = ("z",)
    plane_count, along_count = (lax.axis_size(plane), lax.axis_size(along))
    keep = jnp.where(core == 0, first_total, second_total)
    send = jnp.where(core == 0, second_total, first_total).astype(jnp.bfloat16)
    half = (keep + lax.ppermute(send, "core", swap).astype(jnp.float32)).astype(jnp.bfloat16)
    rows, channels = half.shape
    piece = rows // plane_count
    unit = -(-piece // (16 * along_count)) * 16
    part = summed(exchange(half.reshape(plane_count, piece, channels), plane))
    part = jnp.pad(part, ((0, unit * along_count - piece), (0, 0)))
    part = exchange(part.reshape(along_count, unit, channels), along)
    part = (jnp.sum(part.astype(jnp.float32), axis=0) * scale).astype(jnp.bfloat16)
    part = exchange(shared(part, along_count), along).reshape(-1, channels)[:piece]
    half = exchange(shared(part, plane_count), plane).reshape(rows, channels)
    other = lax.ppermute(half, "core", swap)
    return jnp.where(core == 0, half, other), jnp.where(core == 0, other, half)


def local(features, occupancy, neighbours, first_weight, second_weight, cotangent):
    channels = features.shape[-1]
    extent = features.shape[3]
    slot_count = features.shape[2]
    lookup = neighbours[0, 0]
    live = lookup[:, 13] >= 0
    mask = occupancy_mask(occupancy, jnp.broadcast_to(live[None, None, :], occupancy.shape), extent)
    masked = features * mask[..., None]
    grad_out = cotangent * mask[..., None]
    first_flat = first_weight.reshape(27 * channels, channels)
    second_flat = second_weight.reshape(27 * channels, channels)
    second_back = jnp.transpose(second_weight[::-1], (0, 2, 1)).reshape(27 * channels, channels)
    scale = 1.0 / math.sqrt(extent**3 * slot_count * lax.axis_size(GX) * lax.axis_size(GY))
    patches_in = gather_taps(extend(boundary(masked), lookup))
    pre_first = flat_product(patches_in, first_flat)
    hidden = (jax.nn.silu(pre_first) * mask[..., None]).astype(jnp.bfloat16)
    patches_hidden = gather_taps(extend(boundary(hidden), lookup))
    pre_second = flat_product(patches_hidden, second_flat)
    activations = (pre_second * mask[..., None]).astype(jnp.bfloat16)
    second_total = outer_sum(patches_hidden, grad_out)
    back = flat_product(gather_taps(extend(boundary(grad_out), lookup)), second_back)
    grad_pre = (back * silu_slope(pre_first) * mask[..., None]).astype(jnp.bfloat16)
    first_total = outer_sum(patches_in, grad_pre)
    first_total, second_total = reduced(first_total, second_total, scale)
    first_grad = first_total.reshape(27, channels, channels)
    second_grad = second_total.reshape(27, channels, channels)
    return (activations, first_grad, second_grad)


def solution(mesh):
    fine = Mesh(mesh.devices.reshape(2, 16, 2, 2, 4), GX + GY)
    in_specs = (
        P(GX, GY, None, None, None),
        P(GX, GY, None),
        P(GX, GY, None, None),
        P(),
        P(),
        P(GX, GY, None, None, None),
    )
    out_specs = (P(GX, GY, None, None, None), P(), P())
    return jax.shard_map(local, mesh=fine, in_specs=in_specs, out_specs=out_specs, check_vma=False)
```

```python
import functools
import math

import jax
import jax.numpy as jnp
from jax import lax
from jax.experimental import pallas as pl
from jax.experimental.pallas import tpu as pltpu
from jax.sharding import Mesh
from jax.sharding import PartitionSpec as P

GX = ("x_lo", "z", "core")
GY = ("x_hi", "y")
PLANE = ("x_lo", "x_hi", "y")
ALONG = ("z",)
SWAP = [(0, 1), (1, 0)]
F32 = jnp.float32
BF16 = jnp.bfloat16
E = 8
LIMIT = 48 * 1024 * 1024
VMEM = pl.BlockSpec(memory_space=pltpu.VMEM)
SMEM = pl.BlockSpec(memory_space=pltpu.SMEM)


def column_mask(occupancy, live, x, y):
    layers = lax.broadcasted_iota(jnp.int32, (E, 128), 0)
    bits = jnp.right_shift(jnp.full((E, 128), occupancy[x, y, 0] * live, jnp.int32), layers) & 1
    return bits.astype(F32)


def row_mask(occupancy, live, x):
    return jnp.stack([column_mask(occupancy, live, x, y) for y in range(E)])


def present(neighbours, p, q):
    base = 9 * (p + 1) + 3 * (q + 1)
    return [jnp.where(neighbours[0, 0, 0, base + r] >= 0, 1.0, 0.0).astype(F32) for r in range(3)]


def live_of(neighbours):
    return jnp.where(neighbours[0, 0, 0, 13] >= 0, 1, 0)


def faces_x(features, cotangent, occupancy, neighbours, low, high):
    live = live_of(neighbours)
    for out, rows, edge in ((low, (0, 1), 0), (high, (E - 2, E - 1), E - 1)):
        for i, x in enumerate(rows):
            mask = row_mask(occupancy, live, x)
            out[i] = (features[x, :, 0].astype(F32) * mask).astype(BF16)
            if x == edge:
                out[2] = (cotangent[x, :, 0].astype(F32) * mask).astype(BF16)
                out[3] = mask.astype(BF16)


def faces_y(features, cotangent, occupancy, neighbours, below, above, low, high):
    live = live_of(neighbours)
    for out, first, edge in ((low, 0, 0), (high, E - 2, E - 1)):
        for x in range(E):
            for i in range(2):
                mask = column_mask(occupancy, live, x, first + i)
                out[x + 2, i] = (features[x, first + i, 0].astype(F32) * mask).astype(BF16)
                if first + i == edge:
                    out[x + 2, 2] = (cotangent[x, edge, 0].astype(F32) * mask).astype(BF16)
                    out[x + 2, 3] = mask.astype(BF16)
        for i in range(2):
            out[i, 0:2] = below[i, first : first + 2]
            out[E + 2 + i, 0:2] = above[i, first : first + 2]
        for i in (2, 3):
            out[1, i] = below[i, edge]
            out[E + 2, i] = above[i, edge]
            out[0, i] = jnp.zeros((E, 128), BF16)
            out[E + 3, i] = jnp.zeros((E, 128), BF16)


def spread(store, values, flags, layers):
    rows = lax.broadcasted_iota(jnp.int32, (E, 128), 0)
    down = pltpu.roll(values, 1, 1)
    up = pltpu.roll(values, E - 1, 1)
    for d in layers:
        own = flags[d + 1]
        under = flags[d] if d >= 0 else jnp.zeros((), F32)
        over = flags[d + 2] if d <= 0 else jnp.zeros((), F32)
        store(0, d, down * jnp.where(rows == 0, under, own)[None])
        store(1, d, values * own)
        store(2, d, up * jnp.where(rows == E - 1, over, own)[None])


def for_each_tap(body):
    def step(tap, carry):
        body(tap, tap // 9, (tap // 3) % 3, tap % 3, pl.ds(pl.multiple_of(tap * 128, 128), 128))
        return carry

    lax.fori_loop(0, 27, step, 0)


def gather_own(shifted, patches, first):
    def body(tap, i, j, k, lanes):
        for x in range(E):
            part = shifted(k, first + i + x, pl.ds(first + j, E))
            patches[x * 64 : x * 64 + 64, lanes] = part.reshape(64, 128).astype(BF16)

    return body


def main_kernel(
    features, occupancy, neighbours, first_weight, second_weight, cotangent, below, above, left, right, core,
    keep, send, hidden_out,
    wide, narrow, patches, grad_patches, back_weight, masks, hidden, totals,
):
    live = live_of(neighbours)
    for x in range(E):
        masks[x] = row_mask(occupancy, live, x)

    for p in (-1, 0, 1):
        for q in (-1, 0, 1):
            flags = present(neighbours, p, q)
            count = E if p == 0 else 2
            start = {-1: 0, 0: 2, 1: E + 2}[p]
            columns = {-1: slice(0, 2), 0: slice(2, E + 2), 1: slice(E + 2, E + 4)}[q]

            def wide_row(x, carry, p=p, q=q, flags=flags, start=start, columns=columns):
                if q == -1:
                    values = left[start + x, 0:2].astype(F32)
                elif q == 1:
                    values = right[start + x, 0:2].astype(F32)
                elif p == 0:
                    values = features[x, :, 0].astype(F32) * masks[x]
                else:
                    values = (below if p == -1 else above)[x].astype(F32)

                def store(k, d, tile):
                    wide[k, start + x, columns, d + 1] = tile

                spread(store, values, flags, (-1, 0, 1))
                return carry

            lax.fori_loop(0, count, wide_row, 0)

            count = E if p == 0 else 1
            near = {-1: 0, 0: 1, 1: E + 1}[p]
            columns = {-1: slice(0, 1), 0: slice(1, E + 1), 1: slice(E + 1, E + 2)}[q]

            def narrow_row(x, carry, p=p, q=q, flags=flags, start=near, columns=columns):
                if q == -1:
                    values = left[start + 1 + x, 2:3].astype(F32)
                elif q == 1:
                    values = right[start + 1 + x, 2:3].astype(F32)
                elif p == 0:
                    values = cotangent[x, :, 0].astype(F32) * masks[x]
                else:
                    values = (below if p == -1 else above)[2].astype(F32)

                def store(k, d, tile):
                    narrow[k, start + x, columns] = tile

                spread(store, values, flags, (0,))
                return carry

            lax.fori_loop(0, count, narrow_row, 0)

    def layer_of(p, q):
        flags = present(neighbours, p, q)
        return (1.0 + flags[2] - flags[0]).astype(jnp.int32)

    layer = {(p, q): layer_of(p, q) for p in (-1, 0, 1) for q in (-1, 0, 1)}
    own_rows = gather_own(lambda k, x, ys: wide[k, x, ys, 1], patches, 1)

    def wide_tap(tap, i, j, k, lanes):
        own_rows(tap, i, j, k, lanes)
        edges = (
            wide[k, i, pl.ds(1 + j, E), layer[-1, 0]],
            wide[k, E + 1 + i, pl.ds(1 + j, E), layer[1, 0]],
            wide[k, pl.ds(1 + i, E), j, layer[0, -1]],
            wide[k, pl.ds(1 + i, E), E + 1 + j, layer[0, 1]],
        )
        for n, edge in enumerate(edges):
            patches[512 + 64 * n : 576 + 64 * n, lanes] = edge.reshape(64, 128).astype(BF16)
        corners = [
            wide[k, i + (0 if p < 0 else E + 1), j + (0 if q < 0 else E + 1), layer[p, q]]
            for p in (-1, 1) for q in (-1, 1)
        ]
        patches[768:800, lanes] = jnp.concatenate(corners, axis=0).astype(BF16)

    for_each_tap(wide_tap)

    def narrow_tap(tap, i, j, k, lanes):
        gather_own(lambda k, x, ys: narrow[k, x, ys], grad_patches, 0)(tap, i, j, k, lanes)
        back_weight[:, lanes] = second_weight[26 - tap]

    for_each_tap(narrow_tap)

    pre = jnp.dot(patches[...], first_weight[...], preferred_element_type=F32)
    logistic = jax.nn.sigmoid(pre[:512])
    mask = masks[...].reshape(512, 128)
    own = (pre[:512] * logistic * mask).astype(BF16)
    hidden[1 : E + 1, 1 : E + 1] = own.astype(F32).reshape(E, E, E, 128)
    ring = jax.nn.silu(pre[512:])
    hidden[0, 1 : E + 1] = (ring[0:64].reshape(E, E, 128) * below[3].astype(F32)).astype(BF16).astype(F32)
    hidden[E + 1, 1 : E + 1] = (ring[64:128].reshape(E, E, 128) * above[3].astype(F32)).astype(BF16).astype(F32)
    for x in range(E):
        for y, side, at in ((0, left, 128), (E + 1, right, 192)):
            part = ring[at + 8 * x : at + 8 * x + 8] * side[x + 2, 3].astype(F32)
            hidden[x + 1, y] = part.astype(BF16).astype(F32)
    for n, (x, y) in enumerate(((0, 0), (0, E + 1), (E + 1, 0), (E + 1, E + 1))):
        side = left if y == 0 else right
        part = ring[256 + 8 * n : 264 + 8 * n] * side[x + 1, 3].astype(F32)
        hidden[x, y] = part.astype(BF16).astype(F32)
    hidden_out[...] = hidden[...].astype(BF16)

    slope = logistic * (1.0 + pre[:512] * (1.0 - logistic))
    back = lax.dot_general(
        grad_patches[...], back_weight[...], (((1,), (1,)), ((), ())), preferred_element_type=F32
    )
    grad_pre = (back * slope * mask).astype(BF16)
    first_at = jnp.where(core[0] == 0, 0, 1)
    second = jnp.dot(own.astype(F32).T.astype(BF16), grad_patches[...], preferred_element_type=F32)
    for tap in range(27):
        totals[1 - first_at, tap] = second[:, (26 - tap) * 128 : (27 - tap) * 128]
    first = jnp.dot(grad_pre.astype(F32).T.astype(BF16), patches[0:512], preferred_element_type=F32)
    for tap in range(27):
        totals[first_at, tap] = first[:, tap * 128 : tap * 128 + 128].T

    def out_tap(tap, carry):
        keep[tap] = totals[0, tap]
        send[tap] = totals[1, tap].astype(BF16)
        return carry

    lax.fori_loop(0, 27, out_tap, 0)


def last_kernel(hidden, occupancy, neighbours, second_weight, activations, shifts, patches):
    live = live_of(neighbours)
    for p in (-1, 0, 1):
        for q in (-1, 0, 1):
            flags = present(neighbours, p, q)
            start = {-1: 0, 0: 1, 1: E + 1}[p]
            columns = {-1: slice(0, 1), 0: slice(1, E + 1), 1: slice(E + 1, E + 2)}[q]

            def row(x, carry, flags=flags, start=start, columns=columns):
                def store(k, d, tile):
                    shifts[k, start + x, columns] = tile

                spread(store, hidden[start + x, columns].astype(F32), flags, (0,))
                return carry

            lax.fori_loop(0, E if p == 0 else 1, row, 0)
    for_each_tap(gather_own(lambda k, x, ys: shifts[k, x, ys], patches, 0))
    result = jnp.dot(patches[...], second_weight[...], preferred_element_type=F32)
    for x in range(E):
        part = result[64 * x : 64 * x + 64].reshape(E, E, 128) * row_mask(occupancy, live, x)
        activations[x, :, 0] = part.astype(BF16)


def params():
    return pltpu.CompilerParams(vmem_limit_bytes=LIMIT)


def shape(*dims, dtype=BF16):
    return jax.ShapeDtypeStruct(dims, dtype)


def local_faces_x(features, cotangent, occupancy, neighbours):
    face = shape(4, E, E, 128)
    return pl.pallas_call(
        faces_x, out_shape=(face, face), in_specs=[VMEM, VMEM, SMEM, SMEM], out_specs=(VMEM, VMEM),
        compiler_params=params(), name="faces_x",
    )(features, cotangent, occupancy, neighbours)


def local_faces_y(features, cotangent, occupancy, neighbours, below, above):
    face = shape(E + 4, 4, E, 128)
    return pl.pallas_call(
        faces_y, out_shape=(face, face), in_specs=[VMEM, VMEM, SMEM, SMEM, VMEM, VMEM], out_specs=(VMEM, VMEM),
        compiler_params=params(), name="faces_y",
    )(features, cotangent, occupancy, neighbours, below, above)


def local_main(*operands):
    specs = [VMEM, SMEM, SMEM] + [VMEM] * 7 + [SMEM]
    return pl.pallas_call(
        main_kernel,
        out_shape=(shape(27, 128, 128, dtype=F32), shape(27, 128, 128), shape(E + 2, E + 2, E, 128)),
        in_specs=specs,
        out_specs=(VMEM,) * 3,
        scratch_shapes=[
            pltpu.VMEM((3, E + 4, E + 4, 3, E, 128), F32),
            pltpu.VMEM((3, E + 2, E + 2, E, 128), F32),
            pltpu.VMEM((800, 27 * 128), BF16),
            pltpu.VMEM((512, 27 * 128), BF16),
            pltpu.VMEM((128, 27 * 128), BF16),
            pltpu.VMEM((E, E, E, 128), F32),
            pltpu.VMEM((E + 2, E + 2, E, 128), F32),
            pltpu.VMEM((2, 27, 128, 128), F32),
        ],
        compiler_params=params(),
        cost_estimate=pl.CostEstimate(flops=2 * 2200 * 3456 * 128, bytes_accessed=8000000, transcendentals=100000),
        name="grads",
    )(*operands)


def local_last(hidden, occupancy, neighbours, second_weight):
    return pl.pallas_call(
        last_kernel,
        out_shape=shape(E, E, 1, E, 128),
        in_specs=[VMEM, SMEM, SMEM, VMEM],
        out_specs=VMEM,
        scratch_shapes=[pltpu.VMEM((3, E + 2, E + 2, E, 128), F32), pltpu.VMEM((512, 27 * 128), BF16)],
        compiler_params=params(),
        cost_estimate=pl.CostEstimate(flops=2 * 512 * 3456 * 128, bytes_accessed=2000000, transcendentals=0),
        name="activations",
    )(hidden, occupancy, neighbours, second_weight)


def both_ways(low, high, axis):
    count = lax.axis_size(axis)
    up = [(i, (i + 1) % count) for i in range(count)]
    down = [(j, i) for i, j in up]
    return lax.ppermute(high, axis, up), lax.ppermute(low, axis, down)


def exchange(parts, axes):
    return lax.all_to_all(parts, axes, 0, 0, tiled=True)


def shared(part, count):
    return jnp.broadcast_to(part[None], (count,) + part.shape)


def total_of(keep, send, scale):
    plane_count, along_count = (lax.axis_size(PLANE), lax.axis_size(ALONG))
    got = lax.ppermute(send, "core", SWAP)
    half = (keep + got.astype(F32)).astype(BF16).reshape(-1, 128)
    rows = half.shape[0]
    piece = rows // plane_count
    unit = -(-piece // (16 * along_count)) * 16
    part = exchange(half.reshape(plane_count, piece, 128), PLANE)
    part = jnp.sum(part.astype(F32), axis=0).astype(BF16)
    part = jnp.pad(part, ((0, unit * along_count - piece), (0, 0)))
    part = exchange(part.reshape(along_count, unit, 128), ALONG)
    part = (jnp.sum(part.astype(F32), axis=0) * scale).astype(BF16)
    part = exchange(shared(part, along_count), ALONG).reshape(-1, 128)[:piece]
    half = exchange(shared(part, plane_count), PLANE).reshape(27, 128, 128)
    other = lax.ppermute(half, "core", SWAP)
    first = lax.axis_index("core") == 0
    return jnp.where(first, half, other), jnp.where(first, other, half)


def local(features, occupancy, neighbours, first_weight, second_weight, cotangent):
    low, high = local_faces_x(features, cotangent, occupancy, neighbours)
    below, above = both_ways(low, high, GX)
    low, high = local_faces_y(features, cotangent, occupancy, neighbours, below, above)
    left, right = both_ways(low, high, GY)
    core = lax.axis_index("core").astype(jnp.int32).reshape(1)
    keep, send, hidden = local_main(
        features, occupancy, neighbours, first_weight.reshape(-1, 128), second_weight, cotangent,
        below, above, left, right, core,
    )
    activations = local_last(hidden, occupancy, neighbours, second_weight.reshape(-1, 128))
    scale = 1.0 / math.sqrt(E**3 * lax.axis_size(GX) * lax.axis_size(GY))
    first_grad, second_grad = total_of(keep, send, scale)
    return activations, first_grad, second_grad


def solution(mesh):
    fine = Mesh(mesh.devices.reshape(2, 16, 2, 2, 4), GX + GY)
    field = P(GX, GY, None, None, None)
    in_specs = (field, P(GX, GY, None), P(GX, GY, None, None), P(), P(), field)
    return jax.shard_map(local, mesh=fine, in_specs=in_specs, out_specs=(field, P(), P()), check_vma=False)
```

```python
import functools
import math

import jax
import jax.numpy as jnp
from jax import lax
from jax.experimental import pallas as pl
from jax.experimental.pallas import tpu as pltpu
from jax.sharding import Mesh
from jax.sharding import PartitionSpec as P

GX = ("x_lo", "z_hi", "z_lo", "core")
GY = ("x_hi", "y")
NEAR = ("x_lo", "z_lo", "x_hi", "y")
FAR = ("z_hi",)
SWAP = [(0, 1), (1, 0)]
F32 = jnp.float32
BF16 = jnp.bfloat16
E = 8
LIMIT = 48 * 1024 * 1024
VMEM = pl.BlockSpec(memory_space=pltpu.VMEM)
SMEM = pl.BlockSpec(memory_space=pltpu.SMEM)
HBM = pl.BlockSpec(memory_space=pltpu.HBM)


def bits_of(occupied):
    layers = lax.broadcasted_iota(jnp.int32, (E, 128), 0)
    return (jnp.right_shift(occupied, layers) & 1).astype(F32)


def row_mask(occupied, x):
    return jnp.stack([bits_of(jnp.full((E, 128), occupied(x, y), jnp.int32)) for y in range(E)])


def present(neighbours, p, q):
    base = 9 * (p + 1) + 3 * (q + 1)
    return [jnp.where(neighbours[0, base + r] >= 0, 1.0, 0.0).astype(F32) for r in range(3)]


def live_of(neighbours):
    return jnp.where(neighbours[0, 13] >= 0, 1, 0)


def is_even(axis):
    return lax.rem(lax.axis_index(axis), 2) == 0


def start_all(copies):
    for copy in copies:
        copy.start()
    return copies


def wait_all(copies):
    for copy in copies:
        copy.wait()


def faces_x(
    features, cotangent, occupancy, neighbours, masked, graded, masks, out_a, out_b, own, grads, occupied, table, sems
):
    copies = start_all([
        pltpu.make_async_copy(occupancy, occupied, sems.at[0]),
        pltpu.make_async_copy(neighbours, table, sems.at[1]),
        pltpu.make_async_copy(features, own, sems.at[2]),
        pltpu.make_async_copy(cotangent, grads, sems.at[3]),
    ])
    even = is_even("core")
    wait_all(copies[:2])
    live = live_of(table)
    for x in range(E):
        masks[x] = row_mask(lambda x, y: occupied[x, y] * live, x)
    wait_all(copies[2:])
    for x in range(E):
        masked[x] = (own[x].astype(F32) * masks[x]).astype(BF16)
        graded[x] = (grads[x].astype(F32) * masks[x]).astype(BF16)
    rows = lax.broadcasted_iota(jnp.int32, (E, 128), 0)
    for out, high in ((out_a, jnp.where(even, 1, 0)), (out_b, jnp.where(even, 0, 1))):
        edge = (E - 1) * high
        for i in range(2):
            out[E * i : E * i + E] = masked[(E - 2) * high + i]
        out[16:24] = graded[edge]
        values = jnp.zeros((E, 128), jnp.int32)
        for y in range(E):
            values = jnp.where(rows == y, occupied[edge, y] * live, values)
        out[24] = values.astype(F32).astype(BF16)


def faces_y(masked, graded, masks, from_a, from_b, out_a, out_b):
    even_x = is_even("core")
    even = is_even("y")
    rows = lax.broadcasted_iota(jnp.int32, (E, 128), 0)
    weights = jnp.left_shift(jnp.ones((E, 128), jnp.int32), rows).astype(F32)
    zero = jnp.zeros((E, 128), BF16)
    for out, high in ((out_a, jnp.where(even, 1, 0)), (out_b, jnp.where(even, 0, 1))):
        first, edge = ((E - 2) * high, (E - 1) * high)
        for i in range(2):
            for x in range(E):
                out[12 * i + 2 + x] = masked[x, first + i]
                if i == 0:
                    out[26 + x] = graded[x, edge]
            for x in range(2):
                low_a, low_b = (from_a[E * x + first + i], from_b[E * x + first + i])
                out[12 * i + x] = jnp.where(even_x, low_b, low_a)
                out[12 * i + E + 2 + x] = jnp.where(even_x, low_a, low_b)
        at_a, at_b = (from_a[16 + edge], from_b[16 + edge])
        out[24] = zero
        out[35] = zero
        out[25] = jnp.where(even_x, at_b, at_a)
        out[34] = jnp.where(even_x, at_a, at_b)
        values = jnp.zeros((E, 128), F32)
        for x in range(E):
            values = jnp.where(rows == x, jnp.sum(masks[x, edge] * weights, axis=0, keepdims=True), values)
        out[36] = values.astype(BF16)
        in_a, in_b = (from_a[24].astype(F32), from_b[24].astype(F32))
        corner_a = jnp.sum(jnp.where(rows == edge, in_a, 0.0), axis=0, keepdims=True)
        corner_b = jnp.sum(jnp.where(rows == edge, in_b, 0.0), axis=0, keepdims=True)
        low, above = (jnp.where(even_x, corner_b, corner_a), jnp.where(even_x, corner_a, corner_b))
        out[37] = jnp.where(rows == 0, low, jnp.where(rows == 1, above, 0.0)).astype(BF16)


def spread(store, values, flags, layers):
    rows = lax.broadcasted_iota(jnp.int32, (E, 128), 0)
    down = pltpu.roll(values, 1, 1)
    up = pltpu.roll(values, E - 1, 1)
    for d in layers:
        own = flags[d + 1]
        under = flags[d] if d >= 0 else jnp.zeros((), F32)
        over = flags[d + 2] if d <= 0 else jnp.zeros((), F32)
        store(0, d, down * jnp.where(rows == 0, under, own)[None])
        store(1, d, values * own)
        store(2, d, up * jnp.where(rows == E - 1, over, own)[None])


def spread_window(shifts, neighbours, value_of, width, layers):
    for p in (-1, 0, 1):
        for q in (-1, 0, 1):
            flags = present(neighbours, p, q)
            start = {-1: 0, 0: width, 1: E + width}[p]
            columns = {-1: slice(0, width), 0: slice(width, E + width), 1: slice(E + width, E + 2 * width)}[q]

            def row(x, carry, p=p, q=q, flags=flags, start=start, columns=columns):
                def store(k, d, tile):
                    if len(layers) == 1:
                        shifts[k, start + x, columns] = tile
                    else:
                        shifts[k, start + x, columns, d + 1] = tile

                spread(store, value_of(p, q, x, start + x), flags, layers)
                return carry

            lax.fori_loop(0, E if p == 0 else width, row, 0)


def for_each_tap(body):
    def step(tap, carry):
        body(tap, tap // 9, (tap // 3) % 3, tap % 3, pl.ds(pl.multiple_of(tap * 128, 128), 128))
        return carry

    lax.fori_loop(0, 27, step, 0)


def gather_own(shifts, patches, i, j, k, lanes):
    for x in range(E):
        part = shifts[k, i + x, pl.ds(j, E)]
        patches[x * 64 : x * 64 + 64, lanes] = part.reshape(64, 128).astype(BF16)


def main_kernel(
    masked, graded, masks, neighbours, first_weight, second_weight, x_a, x_b, y_a, y_b,
    keep, send, hidden_out,
    first_taps, second_taps, shifts, grad_shifts, patches, grad_patches, back_weight, table, sems,
):
    copies = start_all([
        pltpu.make_async_copy(neighbours, table, sems.at[0]),
        pltpu.make_async_copy(second_weight, second_taps, sems.at[1]),
        pltpu.make_async_copy(first_weight, first_taps, sems.at[2]),
    ])
    even_x = is_even("core")
    even_y = is_even("y")
    wait_all(copies[:1])

    def masked_at(p, q, x, at):
        if q == -1:
            return jnp.where(even_y, y_b[12 + at + 1], y_a[12 + at + 1]).astype(F32)[None]
        if q == 1:
            return jnp.where(even_y, y_a[at + 1], y_b[at + 1]).astype(F32)[None]
        if p == -1:
            return jnp.where(even_x, x_b[E : 2 * E], x_a[E : 2 * E]).astype(F32)
        if p == 1:
            return jnp.where(even_x, x_a[0:E], x_b[0:E]).astype(F32)
        return masked[x].astype(F32)

    def grad_at(p, q, x, at):
        if q == -1:
            return jnp.where(even_y, y_b[24 + at + 1], y_a[24 + at + 1]).astype(F32)[None]
        if q == 1:
            return jnp.where(even_y, y_a[24 + at + 1], y_b[24 + at + 1]).astype(F32)[None]
        if p == -1:
            return jnp.where(even_x, x_b[16:24], x_a[16:24]).astype(F32)
        if p == 1:
            return jnp.where(even_x, x_a[16:24], x_b[16:24]).astype(F32)
        return graded[x].astype(F32)

    spread_window(shifts, table, masked_at, 1, (0,))
    spread_window(grad_shifts, table, grad_at, 1, (0,))
    wait_all(copies[1:])

    def fill(tap, i, j, k, lanes):
        gather_own(shifts, patches, i, j, k, lanes)
        gather_own(grad_shifts, grad_patches, i, j, k, lanes)
        back_weight[:, lanes] = second_taps[26 - tap]

    for_each_tap(fill)

    pre = jnp.dot(patches[...], first_taps[...], preferred_element_type=F32)
    logistic = jax.nn.sigmoid(pre)
    mask = masks[...].reshape(512, 128)
    hidden = (pre * logistic * mask).astype(BF16)
    hidden_out[...] = hidden.reshape(E, E, E, 128)
    back = lax.dot_general(
        grad_patches[...], back_weight[...], (((1,), (1,)), ((), ())), preferred_element_type=F32
    )
    grad_pre = (back * (logistic * (1.0 + pre * (1.0 - logistic))) * mask).astype(BF16)
    hidden_turned = hidden.astype(F32).T.astype(BF16)
    grad_turned = grad_pre.astype(F32).T.astype(BF16)
    second = jnp.dot(hidden_turned, grad_patches[...], preferred_element_type=F32)
    first = jnp.dot(grad_turned, patches[...], preferred_element_type=F32)
    for tap in range(27):
        first_tap = first[:, tap * 128 : tap * 128 + 128].T
        second_tap = second[:, (26 - tap) * 128 : (27 - tap) * 128]
        keep[tap] = jnp.where(even_x, first_tap, second_tap)
        send[tap] = jnp.where(even_x, second_tap, first_tap).astype(BF16)
    keep[27] = jnp.zeros((128, 128), F32)
    send[27] = jnp.zeros((128, 128), BF16)


def last_kernel(
    masked, masks, neighbours, first_weight, second_weight, x_a, x_b, y_a, y_b, hidden_own,
    activations,
    first_taps, second_taps, wide, hidden, shifts, ring_patches, patches, table, sems,
):
    copies = start_all([
        pltpu.make_async_copy(neighbours, table, sems.at[0]),
        pltpu.make_async_copy(first_weight, first_taps, sems.at[1]),
        pltpu.make_async_copy(second_weight, second_taps, sems.at[2]),
    ])
    even_x = is_even("core")
    even_y = is_even("y")

    def below(tiles):
        return jnp.where(even_x, x_b[tiles], x_a[tiles]).astype(F32)

    def above(tiles):
        return jnp.where(even_x, x_a[tiles], x_b[tiles]).astype(F32)

    def left(tiles):
        return jnp.where(even_y, y_b[tiles], y_a[tiles]).astype(F32)

    def right(tiles):
        return jnp.where(even_y, y_a[tiles], y_b[tiles]).astype(F32)

    def mask_of(tile, row):
        return bits_of(jnp.broadcast_to(tile[row : row + 1], (E, 128)).astype(jnp.int32))

    wait_all(copies[:1])

    def masked_at(p, q, x, at):
        if q != 0:
            side = left if q == -1 else right
            return jnp.stack([side(at), side(12 + at)])
        if p != 0:
            return (below if p == -1 else above)(pl.ds(E * x, E))
        return masked[x].astype(F32)

    spread_window(wide, table, masked_at, 2, (-1, 0, 1))

    def layer_of(p, q):
        flags = present(table, p, q)
        return (1.0 + flags[2] - flags[0]).astype(jnp.int32)

    layer = {(p, q): layer_of(p, q) for p in (-1, 0, 1) for q in (-1, 0, 1)}

    def ring_tap(tap, i, j, k, lanes):
        edges = (
            wide[k, i, pl.ds(1 + j, E), layer[-1, 0]],
            wide[k, E + 1 + i, pl.ds(1 + j, E), layer[1, 0]],
            wide[k, pl.ds(1 + i, E), j, layer[0, -1]],
            wide[k, pl.ds(1 + i, E), E + 1 + j, layer[0, 1]],
        )
        for n, edge in enumerate(edges):
            ring_patches[64 * n : 64 * n + 64, lanes] = edge.reshape(64, 128).astype(BF16)
        corners = [
            wide[k, i + (0 if p < 0 else E + 1), j + (0 if q < 0 else E + 1), layer[p, q]]
            for p in (-1, 1) for q in (-1, 1)
        ]
        ring_patches[256:288, lanes] = jnp.concatenate(corners, axis=0).astype(BF16)

    for_each_tap(ring_tap)
    wait_all(copies[1:])

    ring = jax.nn.silu(jnp.dot(ring_patches[...], first_taps[...], preferred_element_type=F32))
    low, high = (below(24), above(24))
    sides = [(side(36), side(37)) for side in (left, right)]
    for y in range(E):
        hidden[0, y + 1] = (ring[8 * y : 8 * y + 8] * mask_of(low, y)).astype(BF16).astype(F32)
        hidden[E + 1, y + 1] = (ring[64 + 8 * y : 72 + 8 * y] * mask_of(high, y)).astype(BF16).astype(F32)
    for x in range(E):
        hidden[x + 1, 1 : E + 1] = hidden_own[x].astype(F32)
        for n, y in enumerate((0, E + 1)):
            part = ring[128 + 64 * n + 8 * x : 136 + 64 * n + 8 * x] * mask_of(sides[n][0], x)
            hidden[x + 1, y] = part.astype(BF16).astype(F32)
    for m, x in enumerate((0, E + 1)):
        for n, y in enumerate((0, E + 1)):
            at = 256 + 16 * m + 8 * n
            hidden[x, y] = (ring[at : at + 8] * mask_of(sides[n][1], m)).astype(BF16).astype(F32)

    def hidden_at(p, q, x, at):
        columns = {-1: slice(0, 1), 0: slice(1, E + 1), 1: slice(E + 1, E + 2)}[q]
        return hidden[at, columns]

    spread_window(shifts, table, hidden_at, 1, (0,))
    for_each_tap(lambda tap, i, j, k, lanes: gather_own(shifts, patches, i, j, k, lanes))
    result = jnp.dot(patches[...], second_taps[...], preferred_element_type=F32)
    for x in range(E):
        part = result[64 * x : 64 * x + 64].reshape(E, E, 128) * masks[x]
        activations[x] = part.astype(BF16)


def params():
    return pltpu.CompilerParams(vmem_limit_bytes=LIMIT)


def shape(*dims, dtype=BF16):
    return jax.ShapeDtypeStruct(dims, dtype)


def vmem(*dims, dtype=BF16):
    return pltpu.VMEM(dims, dtype)


def held(array):
    return pltpu.with_memory_space_constraint(array, pltpu.HBM)


def local_faces_x(features, cotangent, occupancy, neighbours):
    face, field = (shape(25, E, 128), shape(E, E, E, 128))
    return pl.pallas_call(
        faces_x,
        out_shape=(field, field, shape(E, E, E, 128, dtype=F32), face, face),
        in_specs=[HBM] * 4,
        out_specs=(VMEM,) * 5,
        scratch_shapes=[
            vmem(E, E, E, 128), vmem(E, E, E, 128), pltpu.SMEM((E, E), jnp.int32), pltpu.SMEM((1, 27), jnp.int32),
            pltpu.SemaphoreType.DMA((4,)),
        ],
        compiler_params=params(), name="faces_x",
    )(*map(held, (features, cotangent, occupancy, neighbours)))


def local_faces_y(*operands):
    face = shape(38, E, 128)
    return pl.pallas_call(
        faces_y, out_shape=(face, face), in_specs=[VMEM] * 5, out_specs=(VMEM, VMEM),
        compiler_params=params(), name="faces_y",
    )(*operands)


def local_main(*operands):
    return pl.pallas_call(
        main_kernel,
        out_shape=(shape(28, 128, 128, dtype=F32), shape(28, 128, 128), shape(E, E, E, 128)),
        in_specs=[VMEM] * 3 + [HBM] * 3 + [VMEM] * 4,
        out_specs=(VMEM,) * 3,
        scratch_shapes=[
            vmem(27 * 128, 128), vmem(27, 128, 128),
            vmem(3, E + 2, E + 2, E, 128, dtype=F32), vmem(3, E + 2, E + 2, E, 128, dtype=F32),
            vmem(512, 27 * 128), vmem(512, 27 * 128), vmem(128, 27 * 128),
            pltpu.SMEM((1, 27), jnp.int32), pltpu.SemaphoreType.DMA((3,)),
        ],
        compiler_params=params(),
        cost_estimate=pl.CostEstimate(flops=8 * 512 * 3456 * 128, bytes_accessed=8000000, transcendentals=100000),
        name="grads",
    )(*operands)


def local_last(*operands):
    return pl.pallas_call(
        last_kernel,
        out_shape=shape(E, E, E, 128),
        in_specs=[VMEM] * 2 + [HBM] * 3 + [VMEM] * 5,
        out_specs=VMEM,
        scratch_shapes=[
            vmem(27 * 128, 128), vmem(27 * 128, 128),
            vmem(3, E + 4, E + 4, 3, E, 128, dtype=F32),
            vmem(E + 2, E + 2, E, 128, dtype=F32),
            vmem(3, E + 2, E + 2, E, 128, dtype=F32),
            vmem(288, 27 * 128), vmem(512, 27 * 128),
            pltpu.SMEM((1, 27), jnp.int32), pltpu.SemaphoreType.DMA((3,)),
        ],
        compiler_params=params(),
        cost_estimate=pl.CostEstimate(flops=4 * 800 * 3456 * 128, bytes_accessed=2000000, transcendentals=40000),
        name="activations",
    )(*operands)


def paired(out_a, out_b, axis):
    count = lax.axis_size(axis)
    pairs_a = [(i, i ^ 1) for i in range(count)]
    pairs_b = [(i, ((i - 1) ^ 1) + 1) for i in range(1, count - 1)]
    from_b = lax.ppermute(out_b, axis, pairs_b)
    return lax.ppermute(out_a, axis, pairs_a), from_b


def exchange(parts, axes):
    return lax.all_to_all(parts, axes, 0, 0, tiled=True)


def shared(part, count):
    return jnp.broadcast_to(part[None], (count,) + part.shape)


def summed(parts):
    return jnp.sum(parts.astype(F32), axis=0)


def local(features, occupancy, neighbours, first_weight, second_weight, cotangent):
    features, cotangent = (array.reshape(E, E, E, 128) for array in (features, cotangent))
    occupancy, neighbours = (occupancy.reshape(E, E), neighbours.reshape(1, 27))
    first_taps, second_taps = (weight.reshape(27 * 128, 128) for weight in (first_weight, second_weight))
    masked, graded, masks, *out = local_faces_x(features, cotangent, occupancy, neighbours)
    x_a, x_b = paired(*out, GX)
    y_a, y_b = paired(*local_faces_y(masked, graded, masks, x_a, x_b), GY)
    faces = (x_a, x_b, y_a, y_b)
    keep, send, hidden = local_main(
        masked, graded, masks, *map(held, (neighbours, first_taps, second_weight)), *faces
    )
    activations = local_last(
        masked, masks, *map(held, (neighbours, first_taps, second_taps)), *faces, hidden
    )
    scale = 1.0 / math.sqrt(E**3 * lax.axis_size(GX) * lax.axis_size(GY))
    near, far = (lax.axis_size(NEAR), lax.axis_size(FAR))
    got = lax.ppermute(send, "core", SWAP)
    half = (keep + got.astype(F32)).astype(BF16)
    part = summed(exchange(half.reshape(near, -1, 128), NEAR)).astype(BF16)
    part = summed(exchange(shared(part, far), FAR))
    part, activations = lax.optimization_barrier((part, activations))
    part = (part * scale).astype(BF16)
    half = exchange(shared(part, near), NEAR).reshape(28, 128, 128)
    other = lax.ppermute(half, "core", SWAP)
    first = lax.axis_index("core") == 0
    first_grad = jnp.where(first, half, other)[:27]
    second_grad = jnp.where(first, other, half)[:27]
    return activations.reshape(E, E, 1, E, 128), first_grad, second_grad


def solution(mesh):
    fine = Mesh(mesh.devices.reshape(2, 8, 2, 2, 2, 4), GX + GY)
    field = P(GX, GY, None, None, None)
    in_specs = (field, P(GX, GY, None), P(GX, GY, None, None), P(), P(), field)
    return jax.shard_map(local, mesh=fine, in_specs=in_specs, out_specs=(field, P(), P()), check_vma=False)
```

```python
import functools
import math

import jax
import jax.numpy as jnp
from jax import lax
from jax.experimental import pallas as pl
from jax.experimental.pallas import tpu as pltpu
from jax.sharding import Mesh
from jax.sharding import PartitionSpec as P

GX = ("x_lo", "z_hi", "z_lo", "core")
GY = ("x_hi", "y")
NEAR = ("x_lo", "z_lo", "x_hi", "y")
FAR = ("z_hi",)
SWAP = [(0, 1), (1, 0)]
F32 = jnp.float32
BF16 = jnp.bfloat16
E = 8
LIMIT = 30 * 1024 * 1024
VMEM = pl.BlockSpec(memory_space=pltpu.VMEM)
SMEM = pl.BlockSpec(memory_space=pltpu.SMEM)
HBM = pl.BlockSpec(memory_space=pltpu.HBM)


def bits_of(occupied):
    layers = lax.broadcasted_iota(jnp.int32, (E, 128), 0)
    return (jnp.right_shift(occupied, layers) & 1).astype(F32)


def row_mask(occupied, x):
    return jnp.stack([bits_of(jnp.full((E, 128), occupied(x, y), jnp.int32)) for y in range(E)])


def present(neighbours, p, q):
    base = 9 * (p + 1) + 3 * (q + 1)
    return [jnp.where(neighbours[0, base + r] >= 0, 1.0, 0.0).astype(F32) for r in range(3)]


def live_of(neighbours):
    return jnp.where(neighbours[0, 13] >= 0, 1, 0)


def is_even(axis):
    return lax.rem(lax.axis_index(axis), 2) == 0


def start_all(copies):
    for copy in copies:
        copy.start()
    return copies


def wait_all(copies):
    for copy in copies:
        copy.wait()


def faces_x(
    features, cotangent, occupancy, neighbours, masked, graded, masks, out_b, out_a, own, grads, occupied, table, sems
):
    copies = start_all([
        pltpu.make_async_copy(occupancy, occupied, sems.at[0]),
        pltpu.make_async_copy(neighbours, table, sems.at[1]),
        pltpu.make_async_copy(features, own, sems.at[2]),
        pltpu.make_async_copy(cotangent, grads, sems.at[3]),
    ])
    even = is_even("core")
    wait_all(copies[:2])
    live = live_of(table)
    for x in range(E):
        masks[x] = row_mask(lambda x, y: occupied[x, y] * live, x)
    wait_all(copies[2:])
    for x in range(E):
        masked[x] = (own[x].astype(F32) * masks[x]).astype(BF16)
        graded[x] = (grads[x].astype(F32) * masks[x]).astype(BF16)
    rows = lax.broadcasted_iota(jnp.int32, (E, 128), 0)
    for out, high in ((out_a, jnp.where(even, 1, 0)), (out_b, jnp.where(even, 0, 1))):
        edge = (E - 1) * high
        for i in range(2):
            out[E * i : E * i + E] = masked[(E - 2) * high + i]
        out[16:24] = graded[edge]
        values = jnp.zeros((E, 128), jnp.int32)
        for y in range(E):
            values = jnp.where(rows == y, occupied[edge, y] * live, values)
        out[24] = values.astype(F32).astype(BF16)


def faces_y(masked, graded, masks, from_b, from_a, out_b, out_a):
    even_x = is_even("core")
    even = is_even("y")
    rows = lax.broadcasted_iota(jnp.int32, (E, 128), 0)
    weights = jnp.left_shift(jnp.ones((E, 128), jnp.int32), rows).astype(F32)
    zero = jnp.zeros((E, 128), BF16)
    for out, high in ((out_a, jnp.where(even, 1, 0)), (out_b, jnp.where(even, 0, 1))):
        first, edge = ((E - 2) * high, (E - 1) * high)
        for i in range(2):
            for x in range(E):
                out[12 * i + 2 + x] = masked[x, first + i]
                if i == 0:
                    out[26 + x] = graded[x, edge]
            for x in range(2):
                low_a, low_b = (from_a[E * x + first + i], from_b[E * x + first + i])
                out[12 * i + x] = jnp.where(even_x, low_b, low_a)
                out[12 * i + E + 2 + x] = jnp.where(even_x, low_a, low_b)
        at_a, at_b = (from_a[16 + edge], from_b[16 + edge])
        out[24] = zero
        out[35] = zero
        out[25] = jnp.where(even_x, at_b, at_a)
        out[34] = jnp.where(even_x, at_a, at_b)
        values = jnp.zeros((E, 128), F32)
        for x in range(E):
            values = jnp.where(rows == x, jnp.sum(masks[x, edge] * weights, axis=0, keepdims=True), values)
        out[36] = values.astype(BF16)
        in_a, in_b = (from_a[24].astype(F32), from_b[24].astype(F32))
        corner_a = jnp.sum(jnp.where(rows == edge, in_a, 0.0), axis=0, keepdims=True)
        corner_b = jnp.sum(jnp.where(rows == edge, in_b, 0.0), axis=0, keepdims=True)
        low, above = (jnp.where(even_x, corner_b, corner_a), jnp.where(even_x, corner_a, corner_b))
        out[37] = jnp.where(rows == 0, low, jnp.where(rows == 1, above, 0.0)).astype(BF16)


def spread(store, values, flags, layers):
    rows = lax.broadcasted_iota(jnp.int32, (E, 128), 0)
    down = pltpu.roll(values, 1, 1)
    up = pltpu.roll(values, E - 1, 1)
    for d in layers:
        own = flags[d + 1]
        under = flags[d] if d >= 0 else jnp.zeros((), F32)
        over = flags[d + 2] if d <= 0 else jnp.zeros((), F32)
        store(0, d, down * jnp.where(rows == 0, under, own)[None])
        store(1, d, values * own)
        store(2, d, up * jnp.where(rows == E - 1, over, own)[None])


def spread_window(shifts, neighbours, value_of, width, layers):
    for p in (-1, 0, 1):
        for q in (-1, 0, 1):
            flags = present(neighbours, p, q)
            start = {-1: 0, 0: width, 1: E + width}[p]
            columns = {-1: slice(0, width), 0: slice(width, E + width), 1: slice(E + width, E + 2 * width)}[q]

            def row(x, carry, p=p, q=q, flags=flags, start=start, columns=columns):
                def store(k, d, tile):
                    if len(layers) == 1:
                        shifts[k, start + x, columns] = tile
                    else:
                        shifts[k, start + x, columns, d + 1] = tile

                spread(store, value_of(p, q, x, start + x), flags, layers)
                return carry

            lax.fori_loop(0, E if p == 0 else width, row, 0)


def for_each_tap(body):
    def step(tap, carry):
        body(tap, tap // 9, (tap // 3) % 3, tap % 3, pl.ds(pl.multiple_of(tap * 128, 128), 128))
        return carry

    lax.fori_loop(0, 27, step, 0)


def gather_own(shifts, patches, i, j, k, lanes):
    for x in range(E):
        part = shifts[k, i + x, pl.ds(j, E)]
        patches[x * 64 : x * 64 + 64, lanes] = part.reshape(64, 128).astype(BF16)


def weights_kernel(first_weight, second_weight, first_taps, back_weight, second_taps, sems):
    copies = start_all([
        pltpu.make_async_copy(second_weight, second_taps, sems.at[0]),
        pltpu.make_async_copy(first_weight, first_taps, sems.at[1]),
    ])
    copies[0].wait()

    def turn(tap, i, j, k, lanes):
        back_weight[:, lanes] = second_taps[26 - tap]

    for_each_tap(turn)
    copies[1].wait()


def main_kernel(
    masked, graded, masks, neighbours, first_taps, back_weight, x_b, x_a, y_b, y_a,
    send, hidden_out, factors, patches,
    shifts, grad_shifts, raw, table, sems,
):
    copies = start_all([
        pltpu.make_async_copy(neighbours, table, sems.at[0]),
    ])
    even_x = is_even("core")
    even_y = is_even("y")
    wait_all(copies)

    def masked_at(p, q, x, at):
        if q == -1:
            return jnp.where(even_y, y_b[12 + at + 1], y_a[12 + at + 1]).astype(F32)[None]
        if q == 1:
            return jnp.where(even_y, y_a[at + 1], y_b[at + 1]).astype(F32)[None]
        if p == -1:
            return jnp.where(even_x, x_b[E : 2 * E], x_a[E : 2 * E]).astype(F32)
        if p == 1:
            return jnp.where(even_x, x_a[0:E], x_b[0:E]).astype(F32)
        return masked[x].astype(F32)

    def grad_at(p, q, x, at):
        if q == -1:
            return jnp.where(even_y, y_b[24 + at + 1], y_a[24 + at + 1]).astype(F32)[None]
        if q == 1:
            return jnp.where(even_y, y_a[24 + at + 1], y_b[24 + at + 1]).astype(F32)[None]
        if p == -1:
            return jnp.where(even_x, x_b[16:24], x_a[16:24]).astype(F32)
        if p == 1:
            return jnp.where(even_x, x_a[16:24], x_b[16:24]).astype(F32)
        return graded[x].astype(F32)

    spread_window(shifts, table, masked_at, 1, (0,))
    spread_window(grad_shifts, table, grad_at, 1, (0,))

    def fill(tap, i, j, k, lanes):
        gather_own(shifts, patches.at[0], i, j, k, lanes)
        gather_own(grad_shifts, patches.at[1], i, j, k, lanes)

    for_each_tap(fill)

    pre = jnp.dot(patches[0], first_taps[...], preferred_element_type=F32)
    logistic = jax.nn.sigmoid(pre)
    mask = masks[...].reshape(512, 128)
    hidden = (pre * logistic * mask).astype(BF16)
    hidden_out[...] = hidden.reshape(E, E, E, 128)
    back = lax.dot_general(
        patches[1], back_weight[...], (((1,), (1,)), ((), ())), preferred_element_type=F32
    )
    grad_pre = (back * (logistic * (1.0 + pre * (1.0 - logistic))) * mask).astype(BF16)
    factors[0] = grad_pre.astype(F32).T.astype(BF16)
    factors[1] = hidden.astype(F32).T.astype(BF16)
    taps_of(factors, patches, jnp.where(even_x, 1, 0), send, raw)


def keep_kernel(factors, patches, keep, raw):
    taps_of(factors, patches, jnp.where(is_even("core"), 0, 1), keep, raw)


def taps_of(factors, patches, which, out, raw):
    raw[...] = jnp.dot(factors[which], patches[which], preferred_element_type=F32)

    @pl.when(which == 0)
    def _():
        for tap in range(27):
            out[tap] = raw[:, tap * 128 : tap * 128 + 128].T.astype(out.dtype)

    @pl.when(which == 1)
    def _():
        for tap in range(27):
            out[tap] = raw[:, (26 - tap) * 128 : (27 - tap) * 128].astype(out.dtype)

    out[27] = jnp.zeros((128, 128), out.dtype)


def last_kernel(
    masked, masks, neighbours, first_weight, second_weight, x_b, x_a, y_b, y_a, hidden_own,
    activations,
    first_taps, second_taps, wide, hidden, shifts, ring_patches, patches, table, sems,
):
    copies = start_all([
        pltpu.make_async_copy(neighbours, table, sems.at[0]),
        pltpu.make_async_copy(first_weight, first_taps, sems.at[1]),
        pltpu.make_async_copy(second_weight, second_taps, sems.at[2]),
    ])
    even_x = is_even("core")
    even_y = is_even("y")

    def below(tiles):
        return jnp.where(even_x, x_b[tiles], x_a[tiles]).astype(F32)

    def above(tiles):
        return jnp.where(even_x, x_a[tiles], x_b[tiles]).astype(F32)

    def left(tiles):
        return jnp.where(even_y, y_b[tiles], y_a[tiles]).astype(F32)

    def right(tiles):
        return jnp.where(even_y, y_a[tiles], y_b[tiles]).astype(F32)

    def mask_of(tile, row):
        return bits_of(jnp.broadcast_to(tile[row : row + 1], (E, 128)).astype(jnp.int32))

    wait_all(copies[:1])

    def masked_at(p, q, x, at):
        if q != 0:
            side = left if q == -1 else right
            return jnp.stack([side(at), side(12 + at)])
        if p != 0:
            return (below if p == -1 else above)(pl.ds(E * x, E))
        return masked[x].astype(F32)

    spread_window(wide, table, masked_at, 2, (-1, 0, 1))

    def layer_of(p, q):
        flags = present(table, p, q)
        return (1.0 + flags[2] - flags[0]).astype(jnp.int32)

    layer = {(p, q): layer_of(p, q) for p in (-1, 0, 1) for q in (-1, 0, 1)}

    def ring_tap(tap, i, j, k, lanes):
        edges = (
            wide[k, i, pl.ds(1 + j, E), layer[-1, 0]],
            wide[k, E + 1 + i, pl.ds(1 + j, E), layer[1, 0]],
            wide[k, pl.ds(1 + i, E), j, layer[0, -1]],
            wide[k, pl.ds(1 + i, E), E + 1 + j, layer[0, 1]],
        )
        for n, edge in enumerate(edges):
            ring_patches[64 * n : 64 * n + 64, lanes] = edge.reshape(64, 128).astype(BF16)
        corners = [
            wide[k, i + (0 if p < 0 else E + 1), j + (0 if q < 0 else E + 1), layer[p, q]]
            for p in (-1, 1) for q in (-1, 1)
        ]
        ring_patches[256:288, lanes] = jnp.concatenate(corners, axis=0).astype(BF16)

    for_each_tap(ring_tap)
    wait_all(copies[1:])

    ring = jax.nn.silu(jnp.dot(ring_patches[...], first_taps[...], preferred_element_type=F32))
    low, high = (below(24), above(24))
    sides = [(side(36), side(37)) for side in (left, right)]
    for y in range(E):
        hidden[0, y + 1] = (ring[8 * y : 8 * y + 8] * mask_of(low, y)).astype(BF16).astype(F32)
        hidden[E + 1, y + 1] = (ring[64 + 8 * y : 72 + 8 * y] * mask_of(high, y)).astype(BF16).astype(F32)
    for x in range(E):
        hidden[x + 1, 1 : E + 1] = hidden_own[x].astype(F32)
        for n, y in enumerate((0, E + 1)):
            part = ring[128 + 64 * n + 8 * x : 136 + 64 * n + 8 * x] * mask_of(sides[n][0], x)
            hidden[x + 1, y] = part.astype(BF16).astype(F32)
    for m, x in enumerate((0, E + 1)):
        for n, y in enumerate((0, E + 1)):
            at = 256 + 16 * m + 8 * n
            hidden[x, y] = (ring[at : at + 8] * mask_of(sides[n][1], m)).astype(BF16).astype(F32)

    def hidden_at(p, q, x, at):
        columns = {-1: slice(0, 1), 0: slice(1, E + 1), 1: slice(E + 1, E + 2)}[q]
        return hidden[at, columns]

    spread_window(shifts, table, hidden_at, 1, (0,))
    for_each_tap(lambda tap, i, j, k, lanes: gather_own(shifts, patches, i, j, k, lanes))
    result = jnp.dot(patches[...], second_taps[...], preferred_element_type=F32)
    for x in range(E):
        part = result[64 * x : 64 * x + 64].reshape(E, E, 128) * masks[x]
        activations[x] = part.astype(BF16)


def params():
    return pltpu.CompilerParams(vmem_limit_bytes=LIMIT)


def shape(*dims, dtype=BF16):
    return jax.ShapeDtypeStruct(dims, dtype)


def vmem(*dims, dtype=BF16):
    return pltpu.VMEM(dims, dtype)


def held(array):
    return pltpu.with_memory_space_constraint(array, pltpu.HBM)


def local_faces_x(features, cotangent, occupancy, neighbours):
    face, field = (shape(25, E, 128), shape(E, E, E, 128))
    return pl.pallas_call(
        faces_x,
        out_shape=(field, field, shape(E, E, E, 128, dtype=F32), face, face),
        in_specs=[HBM] * 4,
        out_specs=(VMEM,) * 5,
        scratch_shapes=[
            vmem(E, E, E, 128), vmem(E, E, E, 128), pltpu.SMEM((E, E), jnp.int32), pltpu.SMEM((1, 27), jnp.int32),
            pltpu.SemaphoreType.DMA((4,)),
        ],
        compiler_params=params(), name="faces_x",
    )(*map(held, (features, cotangent, occupancy, neighbours)))


def local_faces_y(*operands):
    face = shape(38, E, 128)
    return pl.pallas_call(
        faces_y, out_shape=(face, face), in_specs=[VMEM] * 5, out_specs=(VMEM, VMEM),
        compiler_params=params(), name="faces_y",
    )(*operands)


def local_weights(first_weight, second_weight):
    return pl.pallas_call(
        weights_kernel,
        out_shape=(shape(27 * 128, 128), shape(128, 27 * 128)),
        in_specs=[HBM] * 2,
        out_specs=(VMEM,) * 2,
        scratch_shapes=[vmem(27, 128, 128), pltpu.SemaphoreType.DMA((2,))],
        compiler_params=params(),
        cost_estimate=pl.CostEstimate(flops=0, bytes_accessed=8000000, transcendentals=0),
        name="weights",
    )(held(first_weight), held(second_weight))


def local_main(*operands):
    return pl.pallas_call(
        main_kernel,
        out_shape=(
            shape(28, 128, 128), shape(E, E, E, 128), shape(2, 128, 512), shape(2, 512, 27 * 128)
        ),
        in_specs=[VMEM] * 3 + [HBM] + [VMEM] * 6,
        out_specs=(VMEM,) * 4,
        scratch_shapes=[
            vmem(3, E + 2, E + 2, E, 128, dtype=F32), vmem(3, E + 2, E + 2, E, 128, dtype=F32),
            vmem(128, 27 * 128, dtype=F32),
            pltpu.SMEM((1, 27), jnp.int32), pltpu.SemaphoreType.DMA((1,)),
        ],
        compiler_params=params(),
        cost_estimate=pl.CostEstimate(flops=8 * 512 * 3456 * 128, bytes_accessed=8000000, transcendentals=100000),
        name="grads",
    )(*operands)


def local_keep(factors, patches):
    return pl.pallas_call(
        keep_kernel,
        out_shape=shape(28, 128, 128, dtype=F32),
        in_specs=[VMEM] * 2,
        out_specs=VMEM,
        scratch_shapes=[vmem(128, 27 * 128, dtype=F32)],
        compiler_params=params(),
        cost_estimate=pl.CostEstimate(flops=8 * 512 * 3456 * 128, bytes_accessed=6000000, transcendentals=0),
        name="kept",
    )(*(pltpu.with_memory_space_constraint(array, pltpu.VMEM) for array in (factors, patches)))


def place_kernel(own, source, *refs):
    first, second, sem = refs[-3:]

    def place(out):
        copy = pltpu.make_async_copy(source.at[pl.ds(0, 27)], out, sem)
        copy.start()
        copy.wait()

    even = is_even("core")

    @pl.when(even if own else jnp.logical_not(even))
    def _():
        place(first)

    @pl.when(jnp.logical_not(even) if own else even)
    def _():
        place(second)


def local_place(source, outs=()):
    gradient = shape(27, 128, 128)
    return pl.pallas_call(
        functools.partial(place_kernel, not outs),
        out_shape=(gradient, gradient),
        in_specs=[pl.BlockSpec(memory_space=pl.ANY)] + [HBM] * len(outs),
        out_specs=(HBM, HBM),
        scratch_shapes=[pltpu.SemaphoreType.DMA(())],
        input_output_aliases={1: 0, 2: 1} if outs else {},
        compiler_params=params(),
        cost_estimate=pl.CostEstimate(flops=0, bytes_accessed=4000000, transcendentals=0),
        name="place_other" if outs else "place_own",
    )(source, *outs)


def local_last(*operands):
    return pl.pallas_call(
        last_kernel,
        out_shape=shape(E, E, E, 128),
        in_specs=[VMEM] * 2 + [HBM] * 3 + [VMEM] * 5,
        out_specs=VMEM,
        scratch_shapes=[
            vmem(27 * 128, 128), vmem(27 * 128, 128),
            vmem(3, E + 4, E + 4, 3, E, 128, dtype=F32),
            vmem(E + 2, E + 2, E, 128, dtype=F32),
            vmem(3, E + 2, E + 2, E, 128, dtype=F32),
            vmem(288, 27 * 128), vmem(512, 27 * 128),
            pltpu.SMEM((1, 27), jnp.int32), pltpu.SemaphoreType.DMA((3,)),
        ],
        compiler_params=params(),
        cost_estimate=pl.CostEstimate(flops=4 * 800 * 3456 * 128, bytes_accessed=2000000, transcendentals=40000),
        name="activations",
    )(*operands)


def paired(out_b, out_a, axis):
    count = lax.axis_size(axis)
    pairs_a = [(i, i ^ 1) for i in range(count)]
    pairs_b = [(i, ((i - 1) ^ 1) + 1) for i in range(1, count - 1)]
    return lax.ppermute(out_b, axis, pairs_b), lax.ppermute(out_a, axis, pairs_a)


def exchange(parts, axes):
    return lax.all_to_all(parts, axes, 0, 0, tiled=True)


def shared(part, count):
    return jnp.broadcast_to(part[None], (count,) + part.shape)


def summed(parts):
    return jnp.sum(parts.astype(F32), axis=0)


def local(features, occupancy, neighbours, first_weight, second_weight, cotangent):
    features, cotangent = (array.reshape(E, E, E, 128) for array in (features, cotangent))
    occupancy, neighbours = (occupancy.reshape(E, E), neighbours.reshape(1, 27))
    first_taps, second_taps = (weight.reshape(27 * 128, 128) for weight in (first_weight, second_weight))
    masked, graded, masks, *out = local_faces_x(features, cotangent, occupancy, neighbours)
    x_b, x_a = paired(*out, GX)
    y_b, y_a = paired(*local_faces_y(masked, graded, masks, x_b, x_a), GY)
    faces = (x_b, x_a, y_b, y_a)
    send, hidden, factors, patches = local_main(
        masked, graded, masks, held(neighbours), *local_weights(first_taps, second_weight), *faces
    )
    activations = local_last(
        masked, masks, *map(held, (neighbours, first_taps, second_taps)), *faces, hidden
    )
    scale = 1.0 / math.sqrt(E**3 * lax.axis_size(GX) * lax.axis_size(GY))
    near, far = (lax.axis_size(NEAR), lax.axis_size(FAR))
    got = lax.ppermute(send, "core", SWAP)
    keep = local_keep(factors, patches)
    half = (keep + got.astype(F32)).astype(BF16)
    part = summed(exchange(half.reshape(near, -1, 128), NEAR)).astype(BF16)
    part = summed(exchange(shared(part, far), FAR))
    part, activations = lax.optimization_barrier((part, activations))
    part = (part * scale).astype(BF16)
    half = exchange(shared(part, near), NEAR).reshape(28, 128, 128)
    other = lax.ppermute(half, "core", SWAP)
    first_grad, second_grad = local_place(other, local_place(half))
    return activations.reshape(E, E, 1, E, 128), first_grad, second_grad


def solution(mesh):
    fine = Mesh(mesh.devices.reshape(2, 8, 2, 2, 2, 4), GX + GY)
    field = P(GX, GY, None, None, None)
    in_specs = (field, P(GX, GY, None), P(GX, GY, None, None), P(), P(), field)
    return jax.shard_map(local, mesh=fine, in_specs=in_specs, out_specs=(field, P(), P()), check_vma=False)
```

```python
import functools
import math

import jax
import jax.numpy as jnp
from jax import lax
from jax.experimental import pallas as pl
from jax.experimental.pallas import tpu as pltpu
from jax.sharding import Mesh
from jax.sharding import PartitionSpec as P

GX = ("x_lo", "z_hi", "z_lo", "core")
GY = ("x_hi", "y")
NEAR = ("x_lo", "z_lo", "x_hi", "y")
FAR = "z_hi"
SWAP = [(0, 1), (1, 0)]
F32 = jnp.float32
BF16 = jnp.bfloat16
E = 8
LIMIT = 30 * 1024 * 1024
VMEM = pl.BlockSpec(memory_space=pltpu.VMEM)
SMEM = pl.BlockSpec(memory_space=pltpu.SMEM)
HBM = pl.BlockSpec(memory_space=pltpu.HBM)


def bits_of(occupied):
    layers = lax.broadcasted_iota(jnp.int32, (E, 128), 0)
    return (jnp.right_shift(occupied, layers) & 1).astype(F32)


def row_mask(occupied, x):
    return jnp.stack([bits_of(jnp.full((E, 128), occupied(x, y), jnp.int32)) for y in range(E)])


def present(neighbours, p, q):
    base = 9 * (p + 1) + 3 * (q + 1)
    return [jnp.where(neighbours[0, base + r] >= 0, 1.0, 0.0).astype(F32) for r in range(3)]


def flags_of(tiles, p, q):
    base = 9 * (p + 1) + 3 * (q + 1)
    return [tiles[base + r] for r in range(3)]


def live_of(neighbours):
    return jnp.where(neighbours[0, 13] >= 0, 1, 0)


def is_even(axis):
    return lax.rem(lax.axis_index(axis), 2) == 0


def start_all(copies):
    for copy in copies:
        copy.start()
    return copies


def wait_all(copies):
    for copy in copies:
        copy.wait()


def swapped(face_b, face_a, axis):
    even = is_even(axis)

    def lower(tile):
        return jnp.where(even, face_b[tile], face_a[tile])

    def higher(tile):
        return jnp.where(even, face_a[tile], face_b[tile])

    return lower, higher


def faces_y(
    features, cotangent, occupancy, neighbours, masked, graded, masks, flags, out_b, out_a, own, grads, occupied, table, sems
):
    copies = start_all([
        pltpu.make_async_copy(occupancy, occupied, sems.at[0]),
        pltpu.make_async_copy(neighbours, table, sems.at[1]),
        pltpu.make_async_copy(features, own, sems.at[2]),
        pltpu.make_async_copy(cotangent, grads, sems.at[3]),
    ])
    even = is_even("y")
    wait_all(copies[:2])
    live = live_of(table)
    for n in range(27):
        flags[n] = jnp.full((E, 128), jnp.where(table[0, n] >= 0, 1.0, 0.0), F32)
    for x in range(E):
        masks[x] = row_mask(lambda x, y: occupied[x, y] * live, x)
    wait_all(copies[2:])
    for x in range(E):
        masked[x] = (own[x].astype(F32) * masks[x]).astype(BF16)
        graded[x] = (grads[x].astype(F32) * masks[x]).astype(BF16)
    rows = lax.broadcasted_iota(jnp.int32, (E, 128), 0)
    for out, high in ((out_b, jnp.where(even, 0, 1)), (out_a, jnp.where(even, 1, 0))):
        first, edge = ((E - 2) * high, (E - 1) * high)
        values = jnp.zeros((E, 128), jnp.int32)
        for x in range(E):
            for i in range(2):
                out[E * i + x] = masked[x, first + i]
            out[16 + x] = graded[x, edge]
            values = jnp.where(rows == x, occupied[x, edge] * live, values)
        out[24] = values.astype(F32).astype(BF16)


def faces_x(masked, graded, masks, y_b, y_a, out_b, out_a):
    even = is_even("core")
    left, right = swapped(y_b, y_a, "y")
    rows = lax.broadcasted_iota(jnp.int32, (E, 128), 0)
    weights = jnp.left_shift(jnp.ones((E, 128), jnp.int32), rows).astype(F32)
    zero = jnp.zeros((E, 128), BF16)

    def row_of(tile, row):
        return jnp.sum(jnp.where(rows == row, tile.astype(F32), 0.0), axis=0, keepdims=True)

    for out, high in ((out_b, jnp.where(even, 0, 1)), (out_a, jnp.where(even, 1, 0))):
        first, edge = ((E - 2) * high, (E - 1) * high)
        for i in range(2):
            out[12 * i + 2 : 12 * i + E + 2] = masked[first + i]
            for y in range(2):
                out[12 * i + y] = left(E * y + first + i)
                out[12 * i + E + 2 + y] = right(E * y + first + i)
        out[24] = zero
        out[25] = left(16 + edge)
        out[26:34] = graded[edge]
        out[34] = right(16 + edge)
        out[35] = zero
        values = jnp.zeros((E, 128), F32)
        for y in range(E):
            values = jnp.where(rows == y, jnp.sum(masks[edge, y] * weights, axis=0, keepdims=True), values)
        out[36] = values.astype(BF16)
        low, high_row = (row_of(left(24), edge), row_of(right(24), edge))
        out[37] = jnp.where(rows == 0, low, jnp.where(rows == 1, high_row, 0.0)).astype(BF16)


def spread(store, values, flags, layers):
    rows = lax.broadcasted_iota(jnp.int32, (E, 128), 0)
    down = pltpu.roll(values, 1, 1)
    up = pltpu.roll(values, E - 1, 1)
    for d in layers:
        own = flags[d + 1]
        under = flags[d] if d >= 0 else jnp.zeros((), F32)
        over = flags[d + 2] if d <= 0 else jnp.zeros((), F32)
        store(0, d, down * jnp.where(rows == 0, under, own)[None])
        store(1, d, values * own)
        store(2, d, up * jnp.where(rows == E - 1, over, own)[None])


def spread_window(shifts, flags_at, value_of, width, layers):
    for p in (-1, 0, 1):
        for q in (-1, 0, 1):
            flags = flags_at(p, q)
            start = {-1: 0, 0: width, 1: E + width}[p]
            columns = {-1: slice(0, width), 0: slice(width, E + width), 1: slice(E + width, E + 2 * width)}[q]

            def row(x, carry, p=p, q=q, flags=flags, start=start, columns=columns):
                def store(k, d, tile):
                    if len(layers) == 1:
                        shifts[k, start + x, columns] = tile
                    else:
                        shifts[k, start + x, columns, d + 1] = tile

                spread(store, value_of(p, q, x, start + x), flags, layers)
                return carry

            lax.fori_loop(0, E if p == 0 else width, row, 0)


def for_each_tap(body):
    def step(tap, carry):
        body(tap, tap // 9, (tap // 3) % 3, tap % 3, pl.ds(pl.multiple_of(tap * 128, 128), 128))
        return carry

    lax.fori_loop(0, 27, step, 0)


SIDE = 9 * 128
LAYERS = (E + 2) * 64


def gather_own(*fields):
    def step(tap, carry):
        lanes = pl.ds(pl.multiple_of(tap * 128, 128), 128)
        for shifts, patches in fields:
            for x in range(E + 2):
                part = shifts[tap % 3, x, pl.ds(tap // 3, E)]
                patches[x * 64 : x * 64 + 64, lanes] = part.reshape(64, 128).astype(BF16)
        return carry

    lax.fori_loop(0, 9, step, 0)


def patch_dot(patches, weights):
    total = None
    for i in range(3):
        part = jnp.dot(
            patches[64 * i : 64 * i + 512], weights[SIDE * i : SIDE * i + SIDE], preferred_element_type=F32
        )
        total = part if total is None else total + part
    return total


def weights_kernel(first_weight, second_weight, first_taps, back_weight, second_taps, sems):
    copies = start_all([
        pltpu.make_async_copy(second_weight, second_taps, sems.at[0]),
        pltpu.make_async_copy(first_weight, first_taps, sems.at[1]),
    ])
    copies[0].wait()

    def turn(tap, i, j, k, lanes):
        back_weight[:, lanes] = second_taps[26 - tap]

    for_each_tap(turn)
    copies[1].wait()


def main_kernel(
    masked, graded, masks, flags, first_taps, back_weight, x_b, x_a, y_b, y_a,
    send, hidden_out, factors, patches,
    shifts, grad_shifts, raw,
):
    even_x = is_even("core")
    below, above = swapped(x_b, x_a, "core")
    left, right = swapped(y_b, y_a, "y")

    def beside(p, q, first):
        columns = {-1: slice(first - 1, first), 0: slice(first, first + E), 1: slice(first + E, first + E + 1)}[q]
        return (below if p == -1 else above)(columns).astype(F32)

    def masked_at(p, q, x, at):
        if p != 0:
            return beside(p, q, 14 if p == -1 else 2)
        if q != 0:
            return (left(E + x) if q == -1 else right(x)).astype(F32)[None]
        return masked[x].astype(F32)

    def grad_at(p, q, x, at):
        if p != 0:
            return beside(p, q, 26)
        if q != 0:
            return (left if q == -1 else right)(16 + x).astype(F32)[None]
        return graded[x].astype(F32)

    spread_window(shifts, lambda p, q: flags_of(flags, p, q), masked_at, 1, (0,))
    spread_window(grad_shifts, lambda p, q: flags_of(flags, p, q), grad_at, 1, (0,))

    gather_own((shifts, patches.at[0]), (grad_shifts, patches.at[1]))

    pre = patch_dot(patches.at[0], first_taps)
    logistic = jax.nn.sigmoid(pre)
    mask = masks[...].reshape(512, 128)
    hidden = (pre * logistic * mask).astype(BF16)
    hidden_out[...] = hidden.reshape(E, E, E, 128)
    back = sum(
        lax.dot_general(
            patches[1, 64 * i : 64 * i + 512], back_weight[:, SIDE * i : SIDE * i + SIDE],
            (((1,), (1,)), ((), ())), preferred_element_type=F32,
        )
        for i in range(3)
    )
    grad_pre = (back * (logistic * (1.0 + pre * (1.0 - logistic))) * mask).astype(BF16)
    factors[0] = grad_pre.astype(F32).T.astype(BF16)
    factors[1] = hidden.astype(F32).T.astype(BF16)
    taps_of(factors, patches, jnp.where(even_x, 1, 0), send, raw)


def keep_kernel(factors, patches, keep, raw):
    taps_of(factors, patches, jnp.where(is_even("core"), 0, 1), keep, raw)


def taps_of(factors, patches, which, out, raw):
    for i in range(3):
        raw[:, SIDE * i : SIDE * i + SIDE] = jnp.dot(
            factors[which], patches[which, 64 * i : 64 * i + 512], preferred_element_type=F32
        )

    @pl.when(which == 0)
    def _():
        for tap in range(27):
            out[tap] = raw[:, tap * 128 : tap * 128 + 128].T.astype(out.dtype)

    @pl.when(which == 1)
    def _():
        for tap in range(27):
            out[tap] = raw[:, (26 - tap) * 128 : (27 - tap) * 128].astype(out.dtype)

    out[27] = jnp.zeros((128, 128), out.dtype)


def last_kernel(
    masked, masks, neighbours, first_weight, second_weight, x_b, x_a, y_b, y_a, hidden_own,
    activations,
    first_taps, second_taps, wide, hidden, shifts, ring_patches, patches, table, sems,
):
    copies = start_all([
        pltpu.make_async_copy(neighbours, table, sems.at[0]),
        pltpu.make_async_copy(first_weight, first_taps, sems.at[1]),
        pltpu.make_async_copy(second_weight, second_taps, sems.at[2]),
    ])
    below, above = swapped(x_b, x_a, "core")
    left, right = swapped(y_b, y_a, "y")

    def mask_of(tile, row):
        return bits_of(jnp.broadcast_to(tile[row : row + 1], (E, 128)).astype(jnp.int32))

    wait_all(copies[:1])

    def masked_at(p, q, x, at):
        if p != 0:
            first, count = {-1: (0, 2), 0: (2, E), 1: (E + 2, 2)}[q]
            return (below if p == -1 else above)(pl.ds(12 * x + first, count)).astype(F32)
        if q != 0:
            side = left if q == -1 else right
            return jnp.stack([side(x), side(E + x)]).astype(F32)
        return masked[x].astype(F32)

    spread_window(wide, lambda p, q: present(table, p, q), masked_at, 2, (-1, 0, 1))

    def layer_of(p, q):
        flags = present(table, p, q)
        return (1.0 + flags[2] - flags[0]).astype(jnp.int32)

    layer = {(p, q): layer_of(p, q) for p in (-1, 0, 1) for q in (-1, 0, 1)}

    def ring_tap(tap, i, j, k, lanes):
        edges = (
            wide[k, i, pl.ds(1 + j, E), layer[-1, 0]],
            wide[k, E + 1 + i, pl.ds(1 + j, E), layer[1, 0]],
            wide[k, pl.ds(1 + i, E), j, layer[0, -1]],
            wide[k, pl.ds(1 + i, E), E + 1 + j, layer[0, 1]],
        )
        for n, edge in enumerate(edges):
            ring_patches[64 * n : 64 * n + 64, lanes] = edge.reshape(64, 128).astype(BF16)
        corners = [
            wide[k, i + (0 if p < 0 else E + 1), j + (0 if q < 0 else E + 1), layer[p, q]]
            for p in (-1, 1) for q in (-1, 1)
        ]
        ring_patches[256:288, lanes] = jnp.concatenate(corners, axis=0).astype(BF16)

    for_each_tap(ring_tap)
    wait_all(copies[1:])

    ring = jax.nn.silu(jnp.dot(ring_patches[...], first_taps[...], preferred_element_type=F32))
    ends = [(end(36).astype(F32), end(37).astype(F32)) for end in (below, above)]
    sides = [side(24).astype(F32) for side in (left, right)]
    for y in range(E):
        for m, x in enumerate((0, E + 1)):
            part = ring[64 * m + 8 * y : 64 * m + 8 * y + 8] * mask_of(ends[m][0], y)
            hidden[x, y + 1] = part.astype(BF16).astype(F32)
    for x in range(E):
        hidden[x + 1, 1 : E + 1] = hidden_own[x].astype(F32)
        for n, y in enumerate((0, E + 1)):
            part = ring[128 + 64 * n + 8 * x : 136 + 64 * n + 8 * x] * mask_of(sides[n], x)
            hidden[x + 1, y] = part.astype(BF16).astype(F32)
    for m, x in enumerate((0, E + 1)):
        for n, y in enumerate((0, E + 1)):
            at = 256 + 16 * m + 8 * n
            hidden[x, y] = (ring[at : at + 8] * mask_of(ends[m][1], n)).astype(BF16).astype(F32)

    def hidden_at(p, q, x, at):
        columns = {-1: slice(0, 1), 0: slice(1, E + 1), 1: slice(E + 1, E + 2)}[q]
        return hidden[at, columns]

    spread_window(shifts, lambda p, q: present(table, p, q), hidden_at, 1, (0,))
    gather_own((shifts, patches))
    result = patch_dot(patches, second_taps)
    for x in range(E):
        part = result[64 * x : 64 * x + 64].reshape(E, E, 128) * masks[x]
        activations[x] = part.astype(BF16)


def params():
    return pltpu.CompilerParams(vmem_limit_bytes=LIMIT)


def shape(*dims, dtype=BF16):
    return jax.ShapeDtypeStruct(dims, dtype)


def vmem(*dims, dtype=BF16):
    return pltpu.VMEM(dims, dtype)


def held(array):
    return pltpu.with_memory_space_constraint(array, pltpu.HBM)


def local_faces_y(features, cotangent, occupancy, neighbours):
    face, field = (shape(25, E, 128), shape(E, E, E, 128))
    return pl.pallas_call(
        faces_y,
        out_shape=(field, field, shape(E, E, E, 128, dtype=F32), shape(27, E, 128, dtype=F32), face, face),
        in_specs=[HBM] * 4,
        out_specs=(VMEM,) * 6,
        scratch_shapes=[
            vmem(E, E, E, 128), vmem(E, E, E, 128), pltpu.SMEM((E, E), jnp.int32), pltpu.SMEM((1, 27), jnp.int32),
            pltpu.SemaphoreType.DMA((4,)),
        ],
        compiler_params=params(), name="faces_y",
    )(*map(held, (features, cotangent, occupancy, neighbours)))


def local_faces_x(*operands):
    face = shape(38, E, 128)
    return pl.pallas_call(
        faces_x, out_shape=(face, face), in_specs=[VMEM] * 5, out_specs=(VMEM, VMEM),
        compiler_params=params(), name="faces_x",
    )(*operands)


def local_weights(first_weight, second_weight):
    return pl.pallas_call(
        weights_kernel,
        out_shape=(shape(27 * 128, 128), shape(128, 27 * 128)),
        in_specs=[HBM] * 2,
        out_specs=(VMEM,) * 2,
        scratch_shapes=[vmem(27, 128, 128), pltpu.SemaphoreType.DMA((2,))],
        compiler_params=params(),
        cost_estimate=pl.CostEstimate(flops=0, bytes_accessed=8000000, transcendentals=0),
        name="weights",
    )(held(first_weight), held(second_weight))


def local_main(*operands):
    return pl.pallas_call(
        main_kernel,
        out_shape=(
            shape(28, 128, 128), shape(E, E, E, 128), shape(2, 128, 512), shape(2, LAYERS, SIDE)
        ),
        in_specs=[VMEM] * 10,
        out_specs=(VMEM,) * 4,
        scratch_shapes=[
            vmem(3, E + 2, E + 2, E, 128, dtype=F32), vmem(3, E + 2, E + 2, E, 128, dtype=F32),
            vmem(128, 27 * 128, dtype=F32),
        ],
        compiler_params=params(),
        cost_estimate=pl.CostEstimate(flops=8 * 512 * 3456 * 128, bytes_accessed=8000000, transcendentals=100000),
        name="grads",
    )(*operands)


def local_keep(factors, patches):
    return pl.pallas_call(
        keep_kernel,
        out_shape=shape(28, 128, 128, dtype=F32),
        in_specs=[VMEM] * 2,
        out_specs=VMEM,
        scratch_shapes=[vmem(128, 27 * 128, dtype=F32)],
        compiler_params=params(),
        cost_estimate=pl.CostEstimate(flops=8 * 512 * 3456 * 128, bytes_accessed=6000000, transcendentals=0),
        name="kept",
    )(*(pltpu.with_memory_space_constraint(array, pltpu.VMEM) for array in (factors, patches)))


def place_kernel(own, source, *refs):
    first, second, sem = refs[-3:]

    def place(out):
        copy = pltpu.make_async_copy(source.at[pl.ds(0, 27)], out, sem)
        copy.start()
        copy.wait()

    even = is_even("core")

    @pl.when(even if own else jnp.logical_not(even))
    def _():
        place(first)

    @pl.when(jnp.logical_not(even) if own else even)
    def _():
        place(second)


def local_place(source, outs=()):
    gradient = shape(27, 128, 128)
    return pl.pallas_call(
        functools.partial(place_kernel, not outs),
        out_shape=(gradient, gradient),
        in_specs=[pl.BlockSpec(memory_space=pl.ANY)] + [HBM] * len(outs),
        out_specs=(HBM, HBM),
        scratch_shapes=[pltpu.SemaphoreType.DMA(())],
        input_output_aliases={1: 0, 2: 1} if outs else {},
        compiler_params=params(),
        cost_estimate=pl.CostEstimate(flops=0, bytes_accessed=4000000, transcendentals=0),
        name="place_other" if outs else "place_own",
    )(source, *outs)


def fold_kernel(parts, out):
    for row in range(0, parts.shape[1], 16):
        rows = slice(row, row + 16)
        total = parts[0, rows].astype(F32)
        for i in range(1, parts.shape[0]):
            total = total + parts[i, rows].astype(F32)
        for i in range(out.shape[0]):
            out[i, rows] = total.astype(BF16)


def local_fold(parts, count):
    return pl.pallas_call(
        fold_kernel,
        out_shape=shape(count, *parts.shape[1:]),
        in_specs=[VMEM],
        out_specs=VMEM,
        compiler_params=params(),
        name="fold",
    )(parts)


def local_last(*operands):
    return pl.pallas_call(
        last_kernel,
        out_shape=shape(E, E, E, 128),
        in_specs=[VMEM] * 2 + [HBM] * 3 + [VMEM] * 5,
        out_specs=VMEM,
        scratch_shapes=[
            vmem(27 * 128, 128), vmem(27 * 128, 128),
            vmem(3, E + 4, E + 4, 3, E, 128, dtype=F32),
            vmem(E + 2, E + 2, E, 128, dtype=F32),
            vmem(3, E + 2, E + 2, E, 128, dtype=F32),
            vmem(288, 27 * 128), vmem(LAYERS, SIDE),
            pltpu.SMEM((1, 27), jnp.int32), pltpu.SemaphoreType.DMA((3,)),
        ],
        compiler_params=params(),
        cost_estimate=pl.CostEstimate(flops=4 * 800 * 3456 * 128, bytes_accessed=2000000, transcendentals=40000),
        name="activations",
    )(*operands)


def paired(out_b, out_a, axis):
    count = lax.axis_size(axis)
    pairs_a = [(i, i ^ 1) for i in range(count)]
    pairs_b = [(i, ((i - 1) ^ 1) + 1) for i in range(1, count - 1)]
    return lax.ppermute(out_b, axis, pairs_b), lax.ppermute(out_a, axis, pairs_a)


def exchange(parts, axes):
    return lax.all_to_all(parts, axes, 0, 0, tiled=True)


def shared(part, count):
    return jnp.broadcast_to(part[None], (count,) + part.shape)


def summed(parts):
    return jnp.sum(parts.astype(F32), axis=0)


def local(features, occupancy, neighbours, first_weight, second_weight, cotangent):
    features, cotangent = (array.reshape(E, E, E, 128) for array in (features, cotangent))
    occupancy, neighbours = (occupancy.reshape(E, E), neighbours.reshape(1, 27))
    first_taps, second_taps = (weight.reshape(27 * 128, 128) for weight in (first_weight, second_weight))
    masked, graded, masks, flags, *out = local_faces_y(features, cotangent, occupancy, neighbours)
    y_b, y_a = paired(*out, GY)
    weights = local_weights(first_taps, second_weight)
    y_b, y_a, *weights = lax.optimization_barrier((y_b, y_a, *weights))
    x_b, x_a = paired(*local_faces_x(masked, graded, masks, y_b, y_a), GX)
    faces = (x_b, x_a, y_b, y_a)
    send, hidden, factors, patches = local_main(
        masked, graded, masks, flags, *weights, *faces
    )
    activations = local_last(
        masked, masks, *map(held, (neighbours, first_taps, second_taps)), *faces, hidden
    )
    scale = 1.0 / math.sqrt(E**3 * lax.axis_size(GX) * lax.axis_size(GY))
    near, far = (lax.axis_size(NEAR), lax.axis_size(FAR))
    got = lax.ppermute(send, "core", SWAP)
    keep = local_keep(factors, patches)
    half = (keep + got.astype(F32)).astype(BF16)
    parts = local_fold(exchange(half.reshape(near, -1, 128), NEAR), far)
    order = [(i + far // 2) % far for i in range(far)]
    part = summed(lax.all_to_all(parts, FAR, 0, 0, axis_index_groups=[order], tiled=True))
    part, activations = lax.optimization_barrier((part, activations))
    part = (part * scale).astype(BF16)
    half = exchange(shared(part, near), NEAR).reshape(28, 128, 128)
    other = lax.ppermute(half, "core", SWAP)
    first_grad, second_grad = local_place(other, local_place(half))
    return activations.reshape(E, E, 1, E, 128), first_grad, second_grad


def solution(mesh):
    fine = Mesh(mesh.devices.reshape(2, 8, 2, 2, 2, 4), GX + GY)
    field = P(GX, GY, None, None, None)
    in_specs = (field, P(GX, GY, None), P(GX, GY, None, None), P(), P(), field)
    return jax.shard_map(local, mesh=fine, in_specs=in_specs, out_specs=(field, P(), P()), check_vma=False)
```
